128 devices in a mesh: occ: 8 (over x, core), aux: 16 (over y, z).
Axes of the slice: x: 4, y: 4, z: 4, core: 2. Of those that a mesh axis runs over, the one named last changes fastest.
Arguments:
- b_factors: bfloat16 [16, 8192, 4096], P(None, ('occ', 'aux')), may hold values from -0.5 to 0.5
- eps_occ: float32 [16], replicated, may hold values from -2 to -0.3
- eps_virt: float32 [4096], replicated, may hold values from 0.3 to 3
- dom_blocks: int32 [16, 6], replicated, may hold values from 0 to 31, as said below
- dom_count: int32 [16], replicated, may hold values from 1 to 6
- partners: int32 [16, 8], replicated, may hold values from 0 to 15, as said below
- pair_count: int32 [16], replicated, may hold values from 1 to 8
Outputs:
- pair_energy: float32 [16, 8], P('aux')
The draws below stay inside these ranges and needn't reach their ends.
Inputs may be any that keep to these rules, and one draw needn't show every extreme that they name: `dom_blocks`: the entries of one row are distinct block numbers. `partners`: the entries of one row are distinct occupied orbitals.
All inputs are finite; a program needn't handle non-finite values.
Results may differ from the reference program's by a relative error of at most 0.0023.
Values may be sent and summed in bfloat16 or wider, within the bound.
No kernel may reach another device: no remote copies, remote signals or barrier semaphores. Data moves between devices by JAX's collectives and lax.ppermute only.
A program may use at most 128 MiB of HBM per device.

```python
import jax
import jax.numpy as jnp
from jax import lax

NAUX = 8192
NV = 4096
BLK = 128
MAXDOM = 6
NPAIR = 8
OCC_WIN = 16
N_OCC = 8


def row_permutations(key, row_total, span, width):
    row_keys = jax.random.split(key, row_total)
    return jax.vmap(lambda row_key: jax.random.permutation(row_key, span)[:width])(row_keys).astype(jnp.int32)


def pin_ends(key, table, span):
    row_total = table.shape[0]
    high_row = jax.random.randint(key, (), 0, row_total)
    low_row = (high_row + 1) % row_total
    row_ids = jnp.arange(row_total, dtype=jnp.int32)
    high_shift = span - 1 - table[high_row, 0]
    low_shift = span - table[low_row, 0]
    shifts = jnp.where(row_ids == high_row, high_shift, jnp.where(row_ids == low_row, low_shift, 0))
    return ((table + shifts[:, None]) % span).astype(jnp.int32)


def pin_counts(key, counts, most):
    row_total = counts.shape[0]
    high_row = jax.random.randint(key, (), 0, row_total)
    low_row = (high_row + 1) % row_total
    row_ids = jnp.arange(row_total, dtype=jnp.int32)
    counts = jnp.where(row_ids == high_row, most, counts)
    return jnp.where(row_ids == low_row, 1, counts).astype(jnp.int32)


def draw_dom_blocks(key, part):
    key = jax.random.fold_in(key, 11)
    first_key, second_key = jax.random.split(key)
    table = row_permutations(first_key, OCC_WIN, NV // BLK, MAXDOM)
    return pin_ends(second_key, table, NV // BLK)


def draw_partners(key, part):
    key = jax.random.fold_in(key, 12)
    first_key, second_key = jax.random.split(key)
    table = row_permutations(first_key, OCC_WIN, OCC_WIN, NPAIR)
    return pin_ends(second_key, table, OCC_WIN)


def draw_dom_count(key, part):
    key = jax.random.fold_in(key, 13)
    first_key, second_key = jax.random.split(key)
    counts = jax.random.randint(first_key, (OCC_WIN,), 1, MAXDOM + 1)
    return pin_counts(second_key, counts, MAXDOM)


def draw_pair_count(key, part):
    key = jax.random.fold_in(key, 14)
    first_key, second_key, third_key = jax.random.split(key, 3)
    modest = jax.random.randint(first_key, (OCC_WIN,), 1, NPAIR // 2 + 1)
    filled = jax.random.randint(second_key, (OCC_WIN,), 0, 4) == 0
    counts = jnp.where(filled, NPAIR, modest)
    return pin_counts(third_key, counts, NPAIR)


def shared_part(key, strength):
    mix_key, sign_key, shape_key = jax.random.split(key, 3)
    segment = jnp.arange(NAUX, dtype=jnp.int32) // (NAUX // 16)
    signs = jnp.where(jax.random.randint(sign_key, (16, 4), 0, 2) == 0, -1.0, 1.0).astype(jnp.float32)
    mixing = jax.random.uniform(mix_key, (NAUX, 4), jnp.float32, 0.5, 1.5) * signs[segment]
    shapes = jax.random.normal(shape_key, (OCC_WIN, 4, NV), jnp.float32)
    total = mixing[None, :, 0, None] * shapes[:, 0, None, :]
    total = total + mixing[None, :, 1, None] * shapes[:, 1, None, :]
    total = total + mixing[None, :, 2, None] * shapes[:, 2, None, :]
    total = total + mixing[None, :, 3, None] * shapes[:, 3, None, :]
    return total * (strength * float(NAUX) ** (-0.25))


def draw_b_factors(key, part):
    key = jax.random.fold_in(key, 15)
    noise_key, common_key = jax.random.split(key, 2)
    spread = 1.68 * float(NAUX * MAXDOM * BLK * MAXDOM * BLK) ** (-0.25)
    values = jnp.clip(jax.random.normal(noise_key, (OCC_WIN, NAUX, NV), jnp.float32), -6.0, 6.0)
    values = values + shared_part(common_key, 0.7)
    return jnp.clip(values * spread, -0.5, 0.5).astype(jnp.bfloat16)


def setup_inputs(seed: int = 0) -> dict:
    key_list = jax.random.split(jax.random.key(seed), 8)
    return {
        "b_factors": draw_b_factors(jax.random.fold_in(key_list[7], 71), 0),
        "eps_occ": jnp.clip(jax.random.uniform(key_list[1], (OCC_WIN,), jnp.float32, -2.0, -0.3), -2.0, -0.3),
        "eps_virt": jnp.clip(jax.random.uniform(key_list[2], (NV,), jnp.float32, 0.3, 3.0), 0.3, 3.0),
        "dom_blocks": draw_dom_blocks(jax.random.fold_in(key_list[7], 71), 0),
        "dom_count": draw_dom_count(jax.random.fold_in(key_list[7], 71), 0),
        "partners": draw_partners(jax.random.fold_in(key_list[7], 71), 0),
        "pair_count": draw_pair_count(jax.random.fold_in(key_list[7], 71), 0),
    }


def reference(b_factors, eps_occ, eps_virt, dom_blocks, dom_count, partners, pair_count):
    occ_total, aux_total, virt_total = b_factors.shape
    block_count = virt_total // BLK
    domain_width = MAXDOM * BLK
    live_slots = jnp.arange(MAXDOM, dtype=jnp.int32)[None, :] < dom_count[:, None]
    blocks = b_factors.reshape(occ_total, aux_total, block_count, BLK)
    indices = dom_blocks[:, None, :, None].astype(jnp.int32)
    picked = jnp.take_along_axis(blocks, indices, axis=2)
    picked = jnp.where(live_slots[:, None, :, None], picked, jnp.zeros((), picked.dtype))
    selected = picked.reshape(occ_total, N_OCC, aux_total // N_OCC, domain_width)
    eps_slot = eps_virt.reshape(block_count, BLK)[dom_blocks].reshape(occ_total, domain_width)

    def one_pair(flat_index):
        first_occ = flat_index // NPAIR
        slot_index = flat_index % NPAIR
        second_occ = partners[first_occ, slot_index]
        left_slab = selected[first_occ].astype(jnp.float32)
        right_slab = selected[second_occ].astype(jnp.float32)
        partials = jnp.einsum("kqa,kqb->kab", left_slab, right_slab, precision=lax.Precision.HIGHEST)
        rounded = lax.optimization_barrier(partials.astype(jnp.bfloat16)).astype(jnp.float32)
        integrals = jnp.sum(rounded, axis=0)
        denominator = eps_slot[first_occ][:, None] + eps_slot[second_occ][None, :] - eps_occ[first_occ] - eps_occ[second_occ]
        energy = -jnp.sum(integrals * integrals / denominator)
        return jnp.where(slot_index < pair_count[first_occ], energy, jnp.zeros((), energy.dtype))

    energies = lax.map(one_pair, jnp.arange(occ_total * NPAIR, dtype=jnp.int32))
    return energies.reshape(occ_total, NPAIR)
```

```python
import functools

import jax
import jax.numpy as jnp
from jax import lax
from jax.experimental import pallas as pl
from jax.experimental.pallas import tpu as pltpu
from jax.sharding import Mesh
from jax.sharding import PartitionSpec as P

BLK = 128
MAXDOM = 6
NPAIR = 8
NOCC = 16
AXES = ("x", "core", "y", "z")
SHARE = ("core", "z")
SUMS = ("x", "y")
NSHARE = 8
NSUM = 16
SIZES = ((48, 64), (56, 72), (56, 96), (64, 96), (64, 128), (72, 160), (96, 576))
MAXTILE = SIZES[-1][1]
NONE = NOCC * NOCC

SMEM = pl.BlockSpec(memory_space=pltpu.SMEM)
VMEM = pl.BlockSpec(memory_space=pltpu.VMEM)
ANY = pl.BlockSpec(memory_space=pl.ANY)


def plan_kernel(count, blocks, partners, pair_count, rank, info, where, what, first, mask):
    def scan(i, total):
        first[i] = total
        mask[i] = 0
        return total + count[i]

    live_blocks = lax.fori_loop(0, NOCC, scan, jnp.int32(0))

    def mark(i, total):
        def slot(p, total):
            j = partners[i, p]
            low, high = jnp.minimum(i, j), jnp.maximum(i, j)
            old = mask[low]
            fresh = 1 - ((old >> high) & 1)
            mask[low] = old | (jnp.int32(1) << high)
            return total + fresh * count[i] * count[j]

        return lax.fori_loop(0, pair_count[i], slot, total)

    tiles = lax.fori_loop(0, NOCC, mark, jnp.int32(0))
    quota = 2 * ((tiles + 2 * NSHARE - 1) // (2 * NSHARE))
    low_tile = rank[0] * quota
    high_tile = jnp.minimum(low_tile + quota, tiles)

    def left(i, start):
        def right(j, start):
            width = count[j]
            size = count[i] * width
            live = ((mask[i] >> j) & 1) == 1

            @pl.when(live & (start < high_tile) & (start + size > low_tile))
            def _():
                def row(s, begin):
                    lo = jnp.maximum(low_tile - begin, 0)
                    hi = jnp.minimum(high_tile - begin, width)

                    def tile(t, _):
                        n = begin + t - low_tile
                        where[n] = (first[i] + s) | ((first[j] + t) << 8)
                        what[n] = (i * NOCC + j) | (blocks[i, s] << 9) | (blocks[j, t] << 14)
                        return 0

                    lax.fori_loop(lo, hi, tile, 0)
                    return begin + width

                lax.fori_loop(0, count[i], row, start)

            return start + jnp.where(live, size, 0)

        return lax.fori_loop(i, NOCC, right, start)

    lax.fori_loop(0, NOCC, left, jnp.int32(0))
    mine = jnp.maximum(high_tile - low_tile, 0)

    @pl.when(mine % 2 == 1)
    def _():
        where[mine] = 0
        what[mine] = NONE

    info[0] = live_blocks
    info[1] = quota
    info[2] = (mine + 1) // 2


def make_plan(count, blocks, partners, pair_count, rank):
    return pl.pallas_call(
        plan_kernel,
        out_shape=(
            jax.ShapeDtypeStruct((8,), jnp.int32),
            jax.ShapeDtypeStruct((MAXTILE,), jnp.int32),
            jax.ShapeDtypeStruct((MAXTILE,), jnp.int32),
        ),
        in_specs=[SMEM] * 5,
        out_specs=(SMEM, SMEM, SMEM),
        scratch_shapes=[pltpu.SMEM((NOCC,), jnp.int32), pltpu.SMEM((NOCC,), jnp.int32)],
        name="plan",
    )(count, blocks, partners, pair_count, rank)


def select_kernel(count, blocks, factors, picked, sems):
    def copy(i, s, n):
        return pltpu.make_async_copy(
            factors.at[i, :, pl.ds(pl.multiple_of(blocks[i, s] * BLK, BLK), BLK)], picked.at[n], sems.at[n]
        )

    def each(act):
        def left(i, n):
            def slot(s, n):
                act(copy(i, s, n))
                return n + 1

            return lax.fori_loop(0, count[i], slot, n)

        lax.fori_loop(0, NOCC, left, jnp.int32(0))

    each(lambda c: c.start())
    each(lambda c: c.wait())


def select(count, blocks, factors, room):
    rows = factors.shape[1]
    return pl.pallas_call(
        select_kernel,
        out_shape=jax.ShapeDtypeStruct((room, rows, BLK), factors.dtype),
        in_specs=[SMEM, SMEM, ANY],
        out_specs=ANY,
        scratch_shapes=[pltpu.SemaphoreType.DMA((room,))],
        name="select",
    )(count, blocks, factors)


def product_kernel(info, where, slabs, out):
    depth = slabs.shape[0] * slabs.shape[2]

    def tile(n):
        code = where[n]
        lhs = slabs[:, code & 255].reshape(depth, BLK)
        rhs = slabs[:, code >> 8].reshape(depth, BLK)
        full = lax.dot_general(lhs, rhs, (((0,), (0,)), ((), ())), preferred_element_type=jnp.float32)
        return full.reshape(NSUM, BLK // NSUM, BLK)

    def step(u, _):
        both = jnp.concatenate([tile(2 * u), tile(2 * u + 1)], axis=1)
        out[:, u] = both.astype(out.dtype)
        return 0

    lax.fori_loop(0, info[2], step, 0)


def products(info, where, slabs, room):
    return pl.pallas_call(
        product_kernel,
        out_shape=jax.ShapeDtypeStruct((NSUM, room // 2, 2 * BLK // NSUM, BLK), jnp.bfloat16),
        in_specs=[SMEM, SMEM, VMEM],
        out_specs=VMEM,
        compiler_params=pltpu.CompilerParams(vmem_limit_bytes=48 * 2**20),
        name="products",
    )(info, where, slabs)


def energy_kernel(info, what, partners, pair_count, eps_occ, parts, eps_rows, eps_lanes, out, acc):
    acc[...] = jnp.zeros_like(acc)
    half = BLK // NSUM

    def step(u, _):
        total = jnp.sum(parts[:, u].astype(jnp.float32), axis=0)
        for k in range(2):
            code = what[2 * u + k]
            pair = code & 511
            real = jnp.minimum(pair, NONE - 1)
            i, j = real // NOCC, real % NOCC
            value = total[k * half : (k + 1) * half]
            bottom = eps_rows[(code >> 9) & 31] + eps_lanes[pl.ds(code >> 14, 1), :] - eps_occ[i] - eps_occ[j]
            acc[pair] += value * value / bottom
        return 0

    lax.fori_loop(0, info[2], step, 0)

    rows = []
    for i in range(NOCC):
        lanes = []
        for p in range(NPAIR):
            j = partners[i, p]
            live = p < pair_count[i]
            pair = jnp.where(live, jnp.minimum(i, j) * NOCC + jnp.maximum(i, j), NONE + 1)
            lanes.append(jnp.sum(acc[pair], axis=0, keepdims=True))
        rows.append(jnp.sum(jnp.concatenate(lanes, axis=0), axis=1)[None, :])
    table = -jnp.concatenate(rows, axis=0)
    out[...] = jnp.concatenate([table, jnp.zeros((NOCC, BLK - NPAIR), jnp.float32)], axis=1)


def energies(info, what, partners, pair_count, eps_occ, parts, eps_rows, eps_lanes):
    return pl.pallas_call(
        energy_kernel,
        out_shape=jax.ShapeDtypeStruct((NOCC, BLK), jnp.float32),
        in_specs=[SMEM] * 5 + [VMEM] * 3,
        out_specs=VMEM,
        scratch_shapes=[pltpu.VMEM((NONE + 8, BLK // NSUM, BLK), jnp.float32)],
        compiler_params=pltpu.CompilerParams(vmem_limit_bytes=48 * 2**20),
        name="energies",
    )(info, what, partners, pair_count, eps_occ, parts, eps_rows, eps_lanes)


def body(b_factors, eps_occ, eps_virt, dom_blocks, dom_count, partners, pair_count):
    rank = lax.axis_index(SHARE).astype(jnp.int32).reshape(1)
    info, where, what = make_plan(dom_count, dom_blocks, partners, pair_count, rank)
    eps_lanes = eps_virt.reshape(-1, BLK)
    half = BLK // NSUM
    eps_rows = lax.dynamic_slice_in_dim(eps_lanes, lax.axis_index(SUMS) * half, half, axis=1)
    eps_rows = jnp.broadcast_to(eps_rows[:, :, None], eps_rows.shape + (BLK,))

    def branch(sizes):
        blocks_room, tiles_room = sizes
        picked = select(dom_count, dom_blocks, b_factors, blocks_room)
        slabs = lax.all_gather(picked, SHARE, axis=0, tiled=False)
        sent = products(info, where, slabs, tiles_room)
        parts = lax.all_to_all(sent, SUMS, split_axis=0, concat_axis=0, tiled=True)
        return energies(info, what, partners, pair_count, eps_occ, parts, eps_rows, eps_lanes)

    fits = [(info[0] <= b) & (info[1] <= t) for b, t in SIZES[:-1]] + [jnp.bool_(True)]
    chosen = jnp.argmax(jnp.stack(fits)).astype(jnp.int32)
    table = lax.switch(chosen, [functools.partial(branch, sizes) for sizes in SIZES])
    device_total = 128
    spread = jnp.broadcast_to(table[None], (device_total // NOCC, NOCC, BLK)).reshape(device_total, BLK)
    came = lax.all_to_all(spread, AXES, split_axis=0, concat_axis=0, tiled=True)
    return jnp.sum(came, axis=0, keepdims=True)[:, :NPAIR]


def solution(mesh):
    fine = Mesh(mesh.devices.reshape(4, 2, 4, 4), AXES)
    return jax.shard_map(
        body,
        mesh=fine,
        in_specs=(P(None, AXES, None), P(), P(), P(), P(), P(), P()),
        out_specs=P(("y", "z"), None),
        check_vma=False,
    )
```

```python
import functools

import jax
import jax.numpy as jnp
from jax import lax
from jax.experimental import pallas as pl
from jax.experimental.pallas import tpu as pltpu
from jax.sharding import Mesh
from jax.sharding import PartitionSpec as P

BLK = 128
MAXDOM = 6
NPAIR = 8
NOCC = 16
AXES = ("x", "core", "y", "z")
SHARE = ("core", "z")
SUMS = ("x", "y")
NSHARE = 8
NSUM = 16
SIZES = ((48, 64), (56, 72), (56, 96), (64, 96), (64, 128), (72, 160), (96, 576))
MAXTILE = SIZES[-1][1]
NONE = NOCC * NOCC

SMEM = pl.BlockSpec(memory_space=pltpu.SMEM)
VMEM = pl.BlockSpec(memory_space=pltpu.VMEM)
ANY = pl.BlockSpec(memory_space=pl.ANY)


def sizes_kernel(count, partners, pair_count, info, first, mask):
    def scan(i, total):
        first[i] = total
        mask[i] = 0
        return total + count[i]

    live_blocks = lax.fori_loop(0, NOCC, scan, jnp.int32(0))

    def mark(i, total):
        def slot(p, total):
            j = partners[p, i]
            low, high = jnp.minimum(i, j), jnp.maximum(i, j)
            old = mask[low]
            mask[low] = old | (jnp.int32(1) << high)
            return total + (1 - ((old >> high) & 1)) * count[i] * count[j]

        return lax.fori_loop(0, pair_count[i], slot, total)

    tiles = lax.fori_loop(0, NOCC, mark, jnp.int32(0))
    quota = 2 * ((tiles + 2 * NSHARE - 1) // (2 * NSHARE))
    branch = jnp.int32(len(SIZES) - 1)
    for n in reversed(range(len(SIZES) - 1)):
        fits = (live_blocks <= SIZES[n][0]) & (quota <= SIZES[n][1])
        branch = jnp.where(fits, n, branch)
    info[0] = branch
    info[1] = quota
    info[2] = tiles


def make_sizes(count, partners, pair_count):
    return pl.pallas_call(
        sizes_kernel,
        out_shape=(
            jax.ShapeDtypeStruct((4,), jnp.int32),
            jax.ShapeDtypeStruct((NOCC,), jnp.int32),
            jax.ShapeDtypeStruct((NOCC,), jnp.int32),
        ),
        in_specs=[SMEM] * 3,
        out_specs=(SMEM, SMEM, SMEM),
        name="sizes",
    )(count, partners, pair_count)


def plan_kernel(info, first, mask, count, blocks, rank, steps, where, what):
    low_tile = rank[0] * info[1]
    high_tile = jnp.minimum(low_tile + info[1], info[2])

    def left(i, start):
        def right(j, start):
            width = count[j]
            size = jnp.where(((mask[i] >> j) & 1) == 1, count[i] * width, 0)

            @pl.when((start < high_tile) & (start + size > low_tile))
            def _():
                def row(s, begin):
                    lo = jnp.maximum(low_tile - begin, 0)
                    hi = jnp.minimum(high_tile - begin, width)

                    def tile(t, _):
                        n = begin + t - low_tile
                        where[n] = (first[i] + s) | ((first[j] + t) << 8)
                        what[n] = (i * NOCC + j) | (blocks[s, i] << 9) | (blocks[t, j] << 14)
                        return 0

                    lax.fori_loop(lo, hi, tile, 0)
                    return begin + width

                lax.fori_loop(0, count[i], row, start)

            return start + size

        return lax.fori_loop(i, NOCC, right, start)

    lax.fori_loop(0, NOCC, left, jnp.int32(0))
    mine = jnp.maximum(high_tile - low_tile, 0)

    @pl.when(mine % 2 == 1)
    def _():
        where[mine] = where[mine - 1]
        what[mine] = NONE

    steps[0] = (mine + 1) // 2


def make_plan(info, first, mask, count, blocks, rank):
    return pl.pallas_call(
        plan_kernel,
        out_shape=(
            jax.ShapeDtypeStruct((1,), jnp.int32),
            jax.ShapeDtypeStruct((MAXTILE,), jnp.int32),
            jax.ShapeDtypeStruct((MAXTILE,), jnp.int32),
        ),
        in_specs=[SMEM] * 6,
        out_specs=(SMEM, SMEM, SMEM),
        cost_estimate=pl.CostEstimate(flops=10**7, bytes_accessed=10**7, transcendentals=0),
        name="plan",
    )(info, first, mask, count, blocks, rank)


def select_kernel(count, blocks, factors, picked, sems):
    def copy(i, s, n):
        return pltpu.make_async_copy(
            factors.at[i, :, pl.ds(pl.multiple_of(blocks[s, i] * BLK, BLK), BLK)], picked.at[n], sems.at[n]
        )

    def each(act):
        def left(i, n):
            def slot(s, n):
                act(copy(i, s, n))
                return n + 1

            return lax.fori_loop(0, count[i], slot, n)

        lax.fori_loop(0, NOCC, left, jnp.int32(0))

    each(lambda c: c.start())
    each(lambda c: c.wait())


def select(count, blocks, factors, room):
    rows = factors.shape[1]
    return pl.pallas_call(
        select_kernel,
        out_shape=jax.ShapeDtypeStruct((room, rows, BLK), factors.dtype),
        in_specs=[SMEM, SMEM, ANY],
        out_specs=VMEM,
        scratch_shapes=[pltpu.SemaphoreType.DMA((room,))],
        compiler_params=pltpu.CompilerParams(vmem_limit_bytes=8 * 2**20),
        name="select",
    )(count, blocks, factors)


def gather(own):
    swap = [(0, 1), (1, 0)]
    around = [(4 * c + z, 4 * c + (z + 1 - 2 * c) % 4) for c in range(2) for z in range(4)]
    twin = lax.ppermute(own, "core", swap)
    near = lax.ppermute(own, SHARE, around)
    near_twin = lax.ppermute(twin, SHARE, around)
    far = lax.ppermute(near, SHARE, around)
    return [own, twin, near, near_twin, far] + [lax.ppermute(a, "core", swap) for a in (near, near_twin, far)]


def product_kernel(steps, where, *refs):
    slabs, out, left = refs[:NSHARE], refs[NSHARE], refs[NSHARE + 1]

    def block(n):
        return jnp.concatenate([slab[n] for slab in slabs], axis=0)

    def tile(n, last):
        code = where[n]
        lhs = code & 255

        @pl.when(lhs != last)
        def _():
            left[...] = block(lhs).T

        full = jnp.dot(left[...], block(code >> 8), preferred_element_type=jnp.float32)
        return full.reshape(NSUM, BLK // NSUM, BLK), lhs

    def step(u, last):
        even, last = tile(2 * u, last)
        odd, last = tile(2 * u + 1, last)
        out[:, u] = jnp.concatenate([even, odd], axis=1).astype(out.dtype)
        return last

    lax.fori_loop(0, steps[0], step, jnp.int32(-1))


def products(steps, where, slabs, room):
    blocks, rows, _ = slabs[0].shape
    need = 2 * (NSHARE * blocks * rows * BLK + room * BLK * BLK) + 4 * 2**20
    return pl.pallas_call(
        product_kernel,
        out_shape=jax.ShapeDtypeStruct((NSUM, room // 2, 2 * BLK // NSUM, BLK), jnp.bfloat16),
        in_specs=[SMEM, SMEM] + [VMEM] * NSHARE,
        out_specs=VMEM,
        scratch_shapes=[pltpu.VMEM((BLK, NSHARE * rows), jnp.bfloat16)],
        compiler_params=pltpu.CompilerParams(vmem_limit_bytes=need),
        name="products",
    )(steps, where, *slabs)


def energy_kernel(steps, what, partners, pair_count, eps_occ, parts, eps_rows, eps_lanes, out, acc):
    acc[...] = jnp.zeros_like(acc)
    half = BLK // NSUM

    def step(u, _):
        total = jnp.sum(parts[:, u].astype(jnp.float32), axis=0)
        for k in range(2):
            code = what[2 * u + k]
            pair = code & 511
            real = jnp.minimum(pair, NONE - 1)
            i, j = real // NOCC, real % NOCC
            value = total[k * half : (k + 1) * half]
            bottom = eps_rows[(code >> 9) & 31] + eps_lanes[pl.ds(code >> 14, 1), :] - eps_occ[i] - eps_occ[j]
            acc[pair] += value * value / bottom
        return 0

    lax.fori_loop(0, steps[0], step, 0)

    rows = []
    for i in range(NOCC):
        lanes = []
        for p in range(NPAIR):
            j = partners[p, i]
            live = p < pair_count[i]
            pair = jnp.where(live, jnp.minimum(i, j) * NOCC + jnp.maximum(i, j), NONE + 1)
            lanes.append(jnp.sum(acc[pair], axis=0, keepdims=True))
        rows.append(jnp.sum(jnp.concatenate(lanes, axis=0), axis=1)[None, :])
    table = -jnp.concatenate(rows, axis=0)
    out[...] = jnp.concatenate([table, jnp.zeros((NOCC, BLK - NPAIR), jnp.float32)], axis=1)


def energies(steps, what, partners, pair_count, eps_occ, parts, eps_rows, eps_lanes):
    return pl.pallas_call(
        energy_kernel,
        out_shape=jax.ShapeDtypeStruct((NOCC, BLK), jnp.float32),
        in_specs=[SMEM] * 5 + [VMEM] * 3,
        out_specs=VMEM,
        scratch_shapes=[pltpu.VMEM((NONE + 8, BLK // NSUM, BLK), jnp.float32)],
        compiler_params=pltpu.CompilerParams(vmem_limit_bytes=2 * parts.size + 6 * 2**20),
        name="energies",
    )(steps, what, partners, pair_count, eps_occ, parts, eps_rows, eps_lanes)


def body(b_factors, eps_occ, eps_virt, dom_blocks, dom_count, partners, pair_count):
    blocks, partners = dom_blocks.T, partners.T
    rank = lax.axis_index(SHARE).astype(jnp.int32).reshape(1)
    info, first, mask = make_sizes(dom_count, partners, pair_count)

    def branch(sizes):
        blocks_room, tiles_room = sizes
        slabs = gather(select(dom_count, blocks, b_factors, blocks_room))
        steps, where, what = make_plan(info, first, mask, dom_count, blocks, rank)
        eps_lanes = eps_virt.reshape(-1, BLK)
        half = BLK // NSUM
        eps_rows = lax.dynamic_slice_in_dim(eps_lanes, lax.axis_index(SUMS) * half, half, axis=1)
        eps_rows = jnp.broadcast_to(eps_rows[:, :, None], eps_rows.shape + (BLK,))
        sent = products(steps, where, slabs, tiles_room)
        parts = lax.all_to_all(sent, SUMS, split_axis=0, concat_axis=0, tiled=True)
        return energies(steps, what, partners, pair_count, eps_occ, parts, eps_rows, eps_lanes)

    table = lax.switch(info[0], [functools.partial(branch, sizes) for sizes in SIZES])
    device_total = 128
    spread = jnp.broadcast_to(table[None], (device_total // NOCC, NOCC, BLK)).reshape(device_total, BLK)
    came = lax.all_to_all(spread, AXES, split_axis=0, concat_axis=0, tiled=True)
    return jnp.sum(came, axis=0, keepdims=True)[:, :NPAIR]


def solution(mesh):
    fine = Mesh(mesh.devices.reshape(4, 2, 4, 4), AXES)
    return jax.shard_map(
        body,
        mesh=fine,
        in_specs=(P(None, AXES, None), P(), P(), P(), P(), P(), P()),
        out_specs=P(("y", "z"), None),
        check_vma=False,
    )
```

```python
import functools

import jax
import jax.numpy as jnp
from jax import lax
from jax.experimental import pallas as pl
from jax.experimental.pallas import tpu as pltpu
from jax.sharding import Mesh
from jax.sharding import PartitionSpec as P

BLK = 128
MAXDOM = 6
NPAIR = 8
NOCC = 16
AXES = ("x", "core", "y", "z")
SHARE = ("core", "z")
NSHARE = 8
RING = 4
NSUM = 16
PART = 2 * BLK // NSUM
SIZES = (
    (48, 72), (52, 80), (48, 104), (56, 80), (52, 112), (56, 112), (60, 96), (60, 128), (64, 112), (64, 144), (72, 176),
    (96, 576),
)
MAXTILE = SIZES[-1][1]
NONE = NOCC * NOCC

SMEM = pl.BlockSpec(memory_space=pltpu.SMEM)
VMEM = pl.BlockSpec(memory_space=pltpu.VMEM)
ANY = pl.BlockSpec(memory_space=pl.ANY)


def sizes_kernel(count, partners, pair_count, info, first, mask):
    def scan(i, total):
        first[i] = total
        mask[i] = 0
        return total + count[i]

    live_blocks = lax.fori_loop(0, NOCC, scan, jnp.int32(0))

    def mark(i, total):
        def slot(p, total):
            j = partners[p, i]
            low, high = jnp.minimum(i, j), jnp.maximum(i, j)
            old = mask[low]
            mask[low] = old | (jnp.int32(1) << high)
            return total + (1 - ((old >> high) & 1)) * count[i] * count[j]

        return lax.fori_loop(0, pair_count[i], slot, total)

    tiles = lax.fori_loop(0, NOCC, mark, jnp.int32(0))
    quota = 4 * ((tiles + 4 * NSHARE - 1) // (4 * NSHARE))
    branch = jnp.int32(len(SIZES) - 1)
    for n in reversed(range(len(SIZES) - 1)):
        fits = (live_blocks <= SIZES[n][0]) & (quota <= SIZES[n][1])
        branch = jnp.where(fits, n, branch)
    info[0] = branch
    info[1] = quota
    info[2] = tiles


def make_sizes(count, partners, pair_count):
    return pl.pallas_call(
        sizes_kernel,
        out_shape=(
            jax.ShapeDtypeStruct((4,), jnp.int32),
            jax.ShapeDtypeStruct((NOCC,), jnp.int32),
            jax.ShapeDtypeStruct((NOCC,), jnp.int32),
        ),
        in_specs=[SMEM] * 3,
        out_specs=(SMEM, SMEM, SMEM),
        name="sizes",
    )(count, partners, pair_count)


def plan_kernel(info, first, mask, count, blocks, rank, steps, where, what):
    low_tile = rank[0] * info[1]
    high_tile = jnp.minimum(low_tile + info[1], info[2])

    def left(i, start):
        def right(j, start):
            width = count[j]
            size = jnp.where(((mask[i] >> j) & 1) == 1, count[i] * width, 0)

            @pl.when((start < high_tile) & (start + size > low_tile))
            def _():
                span = (first[i] << 16) | ((first[i] + count[i] - 1) << 24)

                def row(s, begin):
                    lo = jnp.maximum(low_tile - begin, 0)
                    hi = jnp.minimum(high_tile - begin, width)

                    def tile(t, _):
                        n = begin + t - low_tile
                        where[n] = (first[i] + s) | ((first[j] + t) << 8) | span
                        what[n] = (i * NOCC + j) | (blocks[s, i] << 9) | (blocks[t, j] << 14)
                        return 0

                    lax.fori_loop(lo, hi, tile, 0)
                    return begin + width

                lax.fori_loop(0, count[i], row, start)

            return start + size

        return lax.fori_loop(i, NOCC, right, start)

    lax.fori_loop(0, NOCC, left, jnp.int32(0))
    mine = jnp.maximum(high_tile - low_tile, 0)

    total = (mine + 3) // 4

    def pad(n, _):
        where[n] = where[mine - 1]
        what[n] = NONE
        return 0

    lax.fori_loop(mine, 4 * total, pad, 0)
    steps[0] = total


def make_plan(info, first, mask, count, blocks, rank):
    return pl.pallas_call(
        plan_kernel,
        out_shape=(
            jax.ShapeDtypeStruct((1,), jnp.int32),
            jax.ShapeDtypeStruct((MAXTILE,), jnp.int32),
            jax.ShapeDtypeStruct((MAXTILE,), jnp.int32),
        ),
        in_specs=[SMEM] * 6,
        out_specs=(SMEM, SMEM, SMEM),
        cost_estimate=pl.CostEstimate(flops=10**7, bytes_accessed=10**7, transcendentals=0),
        name="plan",
    )(info, first, mask, count, blocks, rank)


def select_kernel(count, blocks, factors, picked, sems):
    def copy(i, s, n):
        return pltpu.make_async_copy(
            factors.at[i, :, pl.ds(pl.multiple_of(blocks[s, i] * BLK, BLK), BLK)], picked.at[n], sems.at[n]
        )

    def each(act):
        def left(i, n):
            def slot(s, n):
                act(copy(i, s, n))
                return n + 1

            return lax.fori_loop(0, count[i], slot, n)

        lax.fori_loop(0, NOCC, left, jnp.int32(0))

    each(lambda c: c.start())
    each(lambda c: c.wait())


def select(count, blocks, factors, room):
    rows = factors.shape[1]
    return pl.pallas_call(
        select_kernel,
        out_shape=jax.ShapeDtypeStruct((room, rows, BLK), factors.dtype),
        in_specs=[SMEM, SMEM, ANY],
        out_specs=VMEM,
        scratch_shapes=[pltpu.SemaphoreType.DMA((room,))],
        compiler_params=pltpu.CompilerParams(vmem_limit_bytes=8 * 2**20),
        name="select",
    )(count, blocks, factors)


def gather(own, beside):
    swap = [(0, 1), (1, 0)]
    around = [(RING * c + z, RING * c + (z + 1 - 2 * c) % RING) for c in range(2) for z in range(RING)]
    twin = lax.ppermute(own, "core", swap)
    near = lax.ppermute(own, SHARE, around)
    near_twin = lax.ppermute(twin, SHARE, around)
    near, beside = lax.optimization_barrier((near, beside))
    far = lax.ppermute(near, SHARE, around)
    return [own, twin, near, near_twin, far] + [lax.ppermute(a, "core", swap) for a in (near, near_twin, far)], beside


def place(axis):
    core, at = lax.axis_index("core"), lax.axis_index(axis)
    high, mixed = at >> 1, (at >> 1) ^ (at & 1)
    return jnp.where(core == 0, mixed, high), jnp.where(core == 0, high, mixed)


def exchange(values, axis, second):
    axes = tuple(name for name in AXES if name in ("core", axis))
    number = (lambda core, at: 2 * at + core) if axis == "x" else (lambda core, at: RING * core + at)
    pairs = []
    for core in range(2):
        for at in range(RING):
            other = at ^ 1 if core == second else RING - 1 - at
            pairs.append((number(core, at), number(core, other)))
    return lax.ppermute(values, axes, pairs)


def add(*terms):
    return functools.reduce(jnp.add, [t.astype(jnp.float32) for t in terms])


def sum_flow(keep, send, axes):
    first, last = axes
    come = [exchange(send, first, 0)]
    for axis, second in ((first, 1), (last, 0), (last, 1)):
        terms = [keep] + come
        terms = [t[(0,) * (t.ndim - come[-1].ndim)][1] for t in terms]
        come.append(exchange(add(*terms).astype(keep.dtype), axis, second))
    return add(*[t[(0,) * (t.ndim - 3)] for t in [keep] + come])


def product_kernel(steps, where, mine, *refs):
    slabs, outs, left = refs[:NSHARE], refs[NSHARE : NSHARE + 4], refs[NSHARE + 4]
    pairs = steps[0]

    def block(n):
        return jnp.concatenate([slab[n] for slab in slabs], axis=0)

    @pl.when(pairs > 0)
    def _():
        shift = jnp.int32(0)
        shifts = []
        for flow in range(2):
            low = (where[2 * flow * pairs] >> 16) & 255
            high = where[2 * (flow + 1) * pairs - 1] >> 24
            start = shift - low
            rows = mine[2 * flow]

            def turn(n, _, start=start, rows=rows):
                turned = block(n).T
                for g in range(BLK // PART):
                    left[start + n, g ^ rows] = turned[g * PART : (g + 1) * PART]
                return 0

            lax.fori_loop(low, high + 1, turn, 0)
            shifts.append(start)
            shift = shift + high + 1 - low

        def step(u, _):
            for flow in range(2):
                for k in range(2):
                    code = where[2 * (flow * pairs + u) + (k ^ mine[2 * flow + 1])]
                    lhs = left[shifts[flow] + (code & 255)].reshape(BLK, -1)
                    full = jnp.dot(lhs, block((code >> 8) & 255), preferred_element_type=jnp.float32)
                    full = full.reshape(2, 2, 2, PART, BLK).astype(jnp.bfloat16)
                    outs[2 * flow][:, :, k, u] = full[0]
                    outs[2 * flow + 1][:, :, k, u] = full[1]
            return 0

        lax.fori_loop(0, pairs, step, 0)


def products(steps, where, mine, slabs, room):
    blocks, rows, _ = slabs[0].shape
    spare = blocks + 8
    need = 2 * (NSHARE * (blocks + spare) * rows * BLK + room * BLK * BLK) + 4 * 2**20
    half = jax.ShapeDtypeStruct((2, 2, 2, room // 4, PART, BLK), jnp.bfloat16)
    return pl.pallas_call(
        product_kernel,
        out_shape=(half,) * 4,
        in_specs=[SMEM] * 3 + [VMEM] * NSHARE,
        out_specs=(VMEM,) * 4,
        scratch_shapes=[pltpu.VMEM((spare, BLK // PART, PART, NSHARE * rows), jnp.bfloat16)],
        compiler_params=pltpu.CompilerParams(vmem_limit_bytes=need),
        name="products",
    )(steps, where, mine, *slabs)


def energy_kernel(steps, what, mine, partners, pair_count, eps_occ, *refs):
    sums, eps_rows, eps_lanes, out, acc = refs[:2], refs[2:4], refs[4], refs[5], refs[6]
    acc[...] = jnp.zeros_like(acc)
    pairs = steps[0]

    def step(u, _):
        for flow in range(2):
            code = what[2 * (flow * pairs + u) + mine[2 * flow + 1]]
            pair = code & 511
            real = jnp.minimum(pair, NONE - 1)
            i, j = real // NOCC, real % NOCC
            value = sums[flow][u]
            bottom = eps_rows[flow][(code >> 9) & 31] + eps_lanes[pl.ds(code >> 14, 1), :] - eps_occ[i] - eps_occ[j]
            term = value * value / bottom
            acc[pair] += term[: PART // 2] + term[PART // 2 :]
        return 0

    lax.fori_loop(0, pairs, step, 0)

    rows = []
    for i in range(NOCC):
        lanes = []
        for p in range(NPAIR):
            j = partners[p, i]
            live = p < pair_count[i]
            pair = jnp.where(live, jnp.minimum(i, j) * NOCC + jnp.maximum(i, j), NONE + 1)
            lanes.append(jnp.sum(acc[pair], axis=0, keepdims=True))
        rows.append(jnp.sum(jnp.concatenate(lanes, axis=0), axis=1)[None, :])
    table = -jnp.concatenate(rows, axis=0)
    out[...] = jnp.concatenate([table, jnp.zeros((NOCC, BLK - NPAIR), jnp.float32)], axis=1)


def energies(steps, what, mine, partners, pair_count, eps_occ, sums, eps_rows, eps_lanes):
    return pl.pallas_call(
        energy_kernel,
        out_shape=jax.ShapeDtypeStruct((NOCC, BLK), jnp.float32),
        in_specs=[SMEM] * 6 + [VMEM] * 5,
        out_specs=VMEM,
        scratch_shapes=[pltpu.VMEM((NONE + 8, PART // 2, BLK), jnp.float32)],
        compiler_params=pltpu.CompilerParams(vmem_limit_bytes=8 * sums[0].size + 6 * 2**20),
        name="energies",
    )(steps, what, mine, partners, pair_count, eps_occ, *sums, *eps_rows, eps_lanes)


def body(b_factors, eps_occ, eps_virt, dom_blocks, dom_count, partners, pair_count):
    blocks, partners = dom_blocks.T, partners.T
    rank = lax.axis_index(SHARE).astype(jnp.int32).reshape(1)
    info, first, mask = make_sizes(dom_count, partners, pair_count)

    first_x, second_x = place("x")
    first_y, second_y = place("y")
    rows = (4 * first_x + 2 * second_x + first_y, 4 * first_y + 2 * second_y + first_x)
    mine = jnp.stack([rows[0], second_y, rows[1], second_x]).astype(jnp.int32)
    eps_lanes = eps_virt.reshape(-1, BLK)
    eps_parts = eps_virt.reshape(-1, BLK // PART, PART)

    def branch(sizes):
        blocks_room, tiles_room = sizes
        plan = make_plan(info, first, mask, dom_count, blocks, rank)
        eps_rows = []
        for flow in range(2):
            picked = lax.dynamic_index_in_dim(eps_parts, rows[flow], 1, keepdims=False)
            eps_rows.append(jnp.broadcast_to(picked[:, :, None], picked.shape + (BLK,)))
        own = select(dom_count, blocks, b_factors, blocks_room)
        slabs, ((steps, where, what), eps_rows) = gather(own, (plan, eps_rows))
        keep_x, send_x, keep_y, send_y = products(steps, where, mine, slabs, tiles_room)
        sums = [sum_flow(keep_x, send_x, ("x", "y")), sum_flow(keep_y, send_y, ("y", "x"))]
        return energies(steps, what, mine, partners, pair_count, eps_occ, sums, eps_rows, eps_lanes)

    table = lax.switch(info[0], [functools.partial(branch, sizes) for sizes in SIZES])
    device_total = 128
    spread = jnp.broadcast_to(table[None], (device_total // NOCC, NOCC, BLK)).reshape(device_total, BLK)
    came = lax.all_to_all(spread, AXES, split_axis=0, concat_axis=0, tiled=True)
    return jnp.sum(came, axis=0, keepdims=True)[:, :NPAIR]


def solution(mesh):
    fine = Mesh(mesh.devices.reshape(4, 2, 4, 4), AXES)
    return jax.shard_map(
        body,
        mesh=fine,
        in_specs=(P(None, AXES, None), P(), P(), P(), P(), P(), P()),
        out_specs=P(("y", "z"), None),
        check_vma=False,
    )
```

```python
import functools

import jax
import jax.numpy as jnp
from jax import lax
from jax.experimental import pallas as pl
from jax.experimental.pallas import tpu as pltpu
from jax.sharding import Mesh
from jax.sharding import PartitionSpec as P

BLK = 128
MAXDOM = 6
NPAIR = 8
NOCC = 16
AXES = ("x", "core", "y", "z")
SHARE = ("core", "z")
NSHARE = 8
RING = 4
NSUM = 16
PART = 2 * BLK // NSUM
SIZES = ((57, 88), (64, 120), (73, 172), (96, 576))
MAXTILE = SIZES[-1][1]
NONE = NOCC * NOCC

SMEM = pl.BlockSpec(memory_space=pltpu.SMEM)
VMEM = pl.BlockSpec(memory_space=pltpu.VMEM)
ANY = pl.BlockSpec(memory_space=pl.ANY)


def sizes_kernel(count, partners, pair_count, info, first, mask):
    def scan(i, total):
        first[i] = total
        mask[i] = 0
        return total + count[i]

    live_blocks = lax.fori_loop(0, NOCC, scan, jnp.int32(0))

    def mark(i, total):
        def slot(p, total):
            j = partners[p, i]
            low, high = jnp.minimum(i, j), jnp.maximum(i, j)
            old = mask[low]
            mask[low] = old | (jnp.int32(1) << high)
            return total + (1 - ((old >> high) & 1)) * count[i] * count[j]

        return lax.fori_loop(0, pair_count[i], slot, total)

    tiles = lax.fori_loop(0, NOCC, mark, jnp.int32(0))
    quota = 4 * ((tiles + 4 * NSHARE - 1) // (4 * NSHARE))
    branch = jnp.int32(len(SIZES) - 1)
    for n in reversed(range(len(SIZES) - 1)):
        fits = (live_blocks <= SIZES[n][0]) & (quota <= SIZES[n][1])
        branch = jnp.where(fits, n, branch)
    info[0] = branch
    info[1] = quota
    info[2] = tiles


def make_sizes(count, partners, pair_count):
    return pl.pallas_call(
        sizes_kernel,
        out_shape=(
            jax.ShapeDtypeStruct((4,), jnp.int32),
            jax.ShapeDtypeStruct((NOCC,), jnp.int32),
            jax.ShapeDtypeStruct((NOCC,), jnp.int32),
        ),
        in_specs=[SMEM] * 3,
        out_specs=(SMEM, SMEM, SMEM),
        name="sizes",
    )(count, partners, pair_count)


def plan_kernel(info, first, mask, count, blocks, rank, steps, where, what):
    low_tile = rank[0] * info[1]
    high_tile = jnp.minimum(low_tile + info[1], info[2])

    def left(i, start):
        def right(j, start):
            width = count[j]
            size = jnp.where(((mask[i] >> j) & 1) == 1, count[i] * width, 0)

            @pl.when((start < high_tile) & (start + size > low_tile))
            def _():
                span = (first[i] << 16) | ((first[i] + count[i] - 1) << 24)

                def row(s, begin):
                    lo = jnp.maximum(low_tile - begin, 0)
                    hi = jnp.minimum(high_tile - begin, width)

                    def tile(t, _):
                        n = begin + t - low_tile
                        where[n] = (first[i] + s) | ((first[j] + t) << 8) | span
                        what[n] = (i * NOCC + j) | (blocks[s, i] << 9) | (blocks[t, j] << 14)
                        return 0

                    lax.fori_loop(lo, hi, tile, 0)
                    return begin + width

                lax.fori_loop(0, count[i], row, start)

            return start + size

        return lax.fori_loop(i, NOCC, right, start)

    lax.fori_loop(0, NOCC, left, jnp.int32(0))
    mine = jnp.maximum(high_tile - low_tile, 0)

    total = (mine + 3) // 4

    def pad(n, _):
        where[n] = where[mine - 1]
        what[n] = NONE
        return 0

    lax.fori_loop(mine, 4 * total, pad, 0)
    steps[0] = total


def make_plan(info, first, mask, count, blocks, rank):
    return pl.pallas_call(
        plan_kernel,
        out_shape=(
            jax.ShapeDtypeStruct((1,), jnp.int32),
            jax.ShapeDtypeStruct((MAXTILE,), jnp.int32),
            jax.ShapeDtypeStruct((MAXTILE,), jnp.int32),
        ),
        in_specs=[SMEM] * 6,
        out_specs=(SMEM, SMEM, SMEM),
        cost_estimate=pl.CostEstimate(flops=10**7, bytes_accessed=10**7, transcendentals=0),
        name="plan",
    )(info, first, mask, count, blocks, rank)


def select_kernel(count, blocks, factors, picked, sems):
    def copy(i, s, n):
        return pltpu.make_async_copy(
            factors.at[i, :, pl.ds(pl.multiple_of(blocks[s, i] * BLK, BLK), BLK)], picked.at[n], sems.at[n]
        )

    def each(act):
        def left(i, n):
            def slot(s, n):
                act(copy(i, s, n))
                return n + 1

            return lax.fori_loop(0, count[i], slot, n)

        lax.fori_loop(0, NOCC, left, jnp.int32(0))

    each(lambda c: c.start())
    each(lambda c: c.wait())


def select(count, blocks, factors, room):
    rows = factors.shape[1]
    return pl.pallas_call(
        select_kernel,
        out_shape=jax.ShapeDtypeStruct((room, rows, BLK), factors.dtype),
        in_specs=[SMEM, SMEM, ANY],
        out_specs=VMEM,
        scratch_shapes=[pltpu.SemaphoreType.DMA((room,))],
        compiler_params=pltpu.CompilerParams(vmem_limit_bytes=8 * 2**20),
        name="select",
    )(count, blocks, factors)


def gather(own, beside, early):
    swap = [(0, 1), (1, 0)]
    around = [(RING * c + z, RING * c + (z + 1 - 2 * c) % RING) for c in range(2) for z in range(RING)]
    twin = lax.ppermute(own, "core", swap)
    near = lax.ppermute(own, SHARE, around)
    near_twin = lax.ppermute(twin, SHARE, around)
    near, extra = lax.optimization_barrier((near, beside(twin)))
    far = lax.ppermute(near, SHARE, around)
    pieces = [own, twin, near, near_twin, lax.ppermute(near, "core", swap), lax.ppermute(near_twin, "core", swap)]
    done = early(pieces, extra)
    far, done = lax.optimization_barrier((far, done))
    return pieces, [far, lax.ppermute(far, "core", swap)], extra, done


def place(axis):
    core, at = lax.axis_index("core"), lax.axis_index(axis)
    high, mixed = at >> 1, (at >> 1) ^ (at & 1)
    return jnp.where(core == 0, mixed, high), jnp.where(core == 0, high, mixed)


def exchange(values, axis, second):
    axes = tuple(name for name in AXES if name in ("core", axis))
    number = (lambda core, at: 2 * at + core) if axis == "x" else (lambda core, at: RING * core + at)
    pairs = []
    for core in range(2):
        for at in range(RING):
            other = at ^ 1 if core == second else RING - 1 - at
            pairs.append((number(core, at), number(core, other)))
    return lax.ppermute(values, axes, pairs)


def add(*terms):
    return functools.reduce(jnp.add, [t.astype(jnp.float32) for t in terms])


def sum_flow(keep, send, axes):
    first, last = axes
    come = [exchange(send, first, 0)]
    for axis, second in ((first, 1), (last, 0), (last, 1)):
        terms = [keep] + come
        terms = [t[(0,) * (t.ndim - come[-1].ndim)][1] for t in terms]
        come.append(exchange(add(*terms).astype(keep.dtype), axis, second))
    return add(*[t[(0,) * (t.ndim - 3)] for t in [keep] + come])


def product_kernel(flow, count, based, last, steps, where, mine, *refs):
    slabs, refs = refs[:count], refs[count:]
    base, outs, left = refs[:based], refs[based:-1], refs[-1]
    pairs = steps[0]
    begin = 2 * flow * pairs

    def block(n):
        return jnp.concatenate([slab[n] for slab in slabs], axis=0)

    def turn(n, _):
        turned = block(n).T
        for g in range(BLK // PART):
            left[n, g ^ mine[2 * flow]] = turned[g * PART : (g + 1) * PART]
        return 0

    def pair(u):
        for k in range(2):
            code = where[begin + 2 * u + (k ^ mine[2 * flow + 1])]
            lhs = left[code & 255].reshape(BLK, -1)
            full = jnp.dot(lhs, block((code >> 8) & 255), preferred_element_type=jnp.float32)
            if based:
                full += base[0][u, k]
            if last:
                full = full.reshape(2, 2, 2, PART, BLK).astype(jnp.bfloat16)
                outs[0][:, :, k, u] = full[0]
                outs[1][:, :, k, u] = full[1]
            else:
                outs[0][u, k] = full

    def four(m, _):
        for n in range(4):
            pair(4 * m + n)
        return 0

    def one(u, _):
        pair(u)
        return 0

    @pl.when(pairs > 0)
    def _():
        low = (where[begin] >> 16) & 255
        high = where[begin + 2 * pairs - 1] >> 24
        lax.fori_loop(low, high + 1, turn, 0)
        fours = pairs // 4
        lax.fori_loop(0, fours, four, 0)
        lax.fori_loop(4 * fours, pairs, one, 0)


def products(flow, steps, where, mine, slabs, room, base=None, last=True):
    blocks, rows, _ = slabs[0].shape
    pairs = room // 4
    whole = jax.ShapeDtypeStruct((pairs, 2, BLK, BLK), jnp.float32)
    half = jax.ShapeDtypeStruct((2, 2, 2, pairs, PART, BLK), jnp.bfloat16)
    extra = [] if base is None else [base]
    depth = len(slabs) * rows
    need = 2 * 2 * blocks * depth * BLK + 2 * pairs * BLK * BLK * (6 if extra else 2 if last else 4) + 4 * 2**20
    return pl.pallas_call(
        functools.partial(product_kernel, flow, len(slabs), len(extra), last),
        out_shape=(half, half) if last else whole,
        in_specs=[SMEM] * 3 + [VMEM] * (len(slabs) + len(extra)),
        out_specs=(VMEM, VMEM) if last else VMEM,
        scratch_shapes=[pltpu.VMEM((blocks, BLK // PART, PART, depth), jnp.bfloat16)],
        compiler_params=pltpu.CompilerParams(vmem_limit_bytes=need),
        cost_estimate=pl.CostEstimate(
            flops=4 * pairs * BLK * BLK * depth, bytes_accessed=10 * pairs * BLK * BLK, transcendentals=0
        ),
        name="products",
    )(steps, where, mine, *slabs, *extra)


def energy_kernel(steps, what, mine, partners, pair_count, eps_occ, *refs):
    sums, eps_rows, eps_lanes, out, acc = refs[:2], refs[2:4], refs[4], refs[5], refs[6]
    acc[...] = jnp.zeros_like(acc)
    pairs = steps[0]

    def step(u, _):
        for flow in range(2):
            code = what[2 * (flow * pairs + u) + mine[2 * flow + 1]]
            pair = code & 511
            real = jnp.minimum(pair, NONE - 1)
            i, j = real // NOCC, real % NOCC
            value = sums[flow][u]
            bottom = eps_rows[flow][(code >> 9) & 31] + eps_lanes[pl.ds(code >> 14, 1), :] - eps_occ[i] - eps_occ[j]
            term = value * value / bottom
            acc[pair] += term[: PART // 2] + term[PART // 2 :]
        return 0

    lax.fori_loop(0, pairs, step, 0)

    rows = []
    for i in range(NOCC):
        lanes = []
        for p in range(NPAIR):
            j = partners[p, i]
            live = p < pair_count[i]
            pair = jnp.where(live, jnp.minimum(i, j) * NOCC + jnp.maximum(i, j), NONE + 1)
            lanes.append(jnp.sum(acc[pair], axis=0, keepdims=True))
        rows.append(jnp.sum(jnp.concatenate(lanes, axis=0), axis=1)[None, :])
    table = -jnp.concatenate(rows, axis=0)
    out[...] = jnp.concatenate([table, jnp.zeros((NOCC, BLK - NPAIR), jnp.float32)], axis=1)


def energies(steps, what, mine, partners, pair_count, eps_occ, sums, eps_rows, eps_lanes):
    return pl.pallas_call(
        energy_kernel,
        out_shape=jax.ShapeDtypeStruct((NOCC, BLK), jnp.float32),
        in_specs=[SMEM] * 6 + [VMEM] * 5,
        out_specs=VMEM,
        scratch_shapes=[pltpu.VMEM((NONE + 8, PART // 2, BLK), jnp.float32)],
        compiler_params=pltpu.CompilerParams(vmem_limit_bytes=8 * sums[0].size + 6 * 2**20),
        name="energies",
    )(steps, what, mine, partners, pair_count, eps_occ, *sums, *eps_rows, eps_lanes)


def body(b_factors, eps_occ, eps_virt, dom_blocks, dom_count, partners, pair_count):
    blocks, partners = dom_blocks.T, partners.T
    rank = lax.axis_index(SHARE).astype(jnp.int32).reshape(1)
    info, first, mask = make_sizes(dom_count, partners, pair_count)

    first_x, second_x = place("x")
    first_y, second_y = place("y")
    rows = (4 * first_x + 2 * second_x + first_y, 4 * first_y + 2 * second_y + first_x)
    mine = jnp.stack([rows[0], second_y, rows[1], second_x]).astype(jnp.int32)
    eps_lanes = eps_virt.reshape(-1, BLK)

    def branch(sizes):
        blocks_room, tiles_room = sizes
        split = tiles_room < 256

        def beside(twin):
            info_then, _ = lax.optimization_barrier((info, twin))
            plan = make_plan(info_then, first, mask, dom_count, blocks, rank)
            eps_rows = [lax.dynamic_slice_in_dim(eps_lanes, r * PART, PART, axis=1) for r in rows]
            return plan, [jnp.broadcast_to(e[:, :, None], e.shape + (BLK,)) for e in eps_rows]

        def early(pieces, extra):
            (steps, where, _), _ = extra
            if not split:
                return [None, None]
            return [products(f, steps, where, mine, pieces, tiles_room, last=False) for f in range(2)]

        own = select(dom_count, blocks, b_factors, blocks_room)
        pieces, late, ((steps, where, what), eps_rows), done = gather(own, beside, early)
        late = late if split else pieces + late
        sums = []
        for flow, axes in enumerate((("x", "y"), ("y", "x"))):
            keep, send = products(flow, steps, where, mine, late, tiles_room, base=done[flow])
            sums.append(sum_flow(keep, send, axes))
        return energies(steps, what, mine, partners, pair_count, eps_occ, sums, eps_rows, eps_lanes)

    table = lax.switch(info[0], [functools.partial(branch, sizes) for sizes in SIZES])
    device_total = 128
    spread = jnp.broadcast_to(table[None], (device_total // NOCC, NOCC, BLK)).reshape(device_total, BLK)
    came = lax.all_to_all(spread, AXES, split_axis=0, concat_axis=0, tiled=True)
    return jnp.sum(came, axis=0, keepdims=True)[:, :NPAIR]


def solution(mesh):
    fine = Mesh(mesh.devices.reshape(4, 2, 4, 4), AXES)
    return jax.shard_map(
        body,
        mesh=fine,
        in_specs=(P(None, AXES, None), P(), P(), P(), P(), P(), P()),
        out_specs=P(("y", "z"), None),
        check_vma=False,
    )
```

```python
import functools

import jax
import jax.numpy as jnp
from jax import lax
from jax.experimental import pallas as pl
from jax.experimental.pallas import tpu as pltpu
from jax.sharding import Mesh
from jax.sharding import PartitionSpec as P

BLK = 128
MAXDOM = 6
NPAIR = 8
NOCC = 16
AXES = ("x", "core", "y", "z")
SHARE = ("core", "z")
NSHARE = 8
RING = 4
NSUM = 16
PART = 2 * BLK // NSUM
SIZES = ((57, 88), (64, 120), (73, 172), (96, 576))
MAXTILE = SIZES[-1][1]
UNROLL = 4
NONE = NOCC * NOCC

SMEM = pl.BlockSpec(memory_space=pltpu.SMEM)
VMEM = pl.BlockSpec(memory_space=pltpu.VMEM)
ANY = pl.BlockSpec(memory_space=pl.ANY)


def sizes_kernel(count, partners, pair_count, info, first, mask):
    def scan(i, total):
        first[i] = total
        mask[i] = 0
        return total + count[i]

    live_blocks = lax.fori_loop(0, NOCC, scan, jnp.int32(0))

    def mark(i, total):
        def slot(p, total):
            j = partners[p, i]
            low, high = jnp.minimum(i, j), jnp.maximum(i, j)
            old = mask[low]
            mask[low] = old | (jnp.int32(1) << high)
            return total + (1 - ((old >> high) & 1)) * count[i] * count[j]

        return lax.fori_loop(0, pair_count[i], slot, total)

    tiles = lax.fori_loop(0, NOCC, mark, jnp.int32(0))
    quota = 4 * ((tiles + 4 * NSHARE - 1) // (4 * NSHARE))
    branch = jnp.int32(len(SIZES) - 1)
    for n in reversed(range(len(SIZES) - 1)):
        fits = (live_blocks <= SIZES[n][0]) & (quota <= SIZES[n][1])
        branch = jnp.where(fits, n, branch)
    info[0] = branch
    info[1] = quota
    info[2] = tiles


def make_sizes(count, partners, pair_count):
    return pl.pallas_call(
        sizes_kernel,
        out_shape=(
            jax.ShapeDtypeStruct((4,), jnp.int32),
            jax.ShapeDtypeStruct((NOCC,), jnp.int32),
            jax.ShapeDtypeStruct((NOCC,), jnp.int32),
        ),
        in_specs=[SMEM] * 3,
        out_specs=(SMEM, SMEM, SMEM),
        name="sizes",
    )(count, partners, pair_count)


def plan_kernel(info, first, mask, count, blocks, rank, steps, where, what):
    low_tile = rank[0] * info[1]
    high_tile = jnp.minimum(low_tile + info[1], info[2])

    def left(i, start):
        def right(j, start):
            width = count[j]
            size = jnp.where(((mask[i] >> j) & 1) == 1, count[i] * width, 0)

            @pl.when((start < high_tile) & (start + size > low_tile))
            def _():
                span = (first[i] << 16) | ((first[i] + count[i] - 1) << 24)

                def row(s, begin):
                    lo = jnp.maximum(low_tile - begin, 0)
                    hi = jnp.minimum(high_tile - begin, width)

                    def tile(t, _):
                        n = begin + t - low_tile
                        where[n] = (first[i] + s) | ((first[j] + t) << 8) | span
                        what[n] = (i * NOCC + j) | (blocks[s, i] << 9) | (blocks[t, j] << 14)
                        return 0

                    lax.fori_loop(lo, hi, tile, 0)
                    return begin + width

                lax.fori_loop(0, count[i], row, start)

            return start + size

        return lax.fori_loop(i, NOCC, right, start)

    lax.fori_loop(0, NOCC, left, jnp.int32(0))
    mine = jnp.maximum(high_tile - low_tile, 0)

    total = (mine + 3) // 4

    def pad(n, _):
        where[n] = where[mine - 1]
        what[n] = NONE
        return 0

    lax.fori_loop(mine, 4 * total, pad, 0)
    steps[0] = total


def make_plan(info, first, mask, count, blocks, rank):
    return pl.pallas_call(
        plan_kernel,
        out_shape=(
            jax.ShapeDtypeStruct((1,), jnp.int32),
            jax.ShapeDtypeStruct((MAXTILE,), jnp.int32),
            jax.ShapeDtypeStruct((MAXTILE,), jnp.int32),
        ),
        in_specs=[SMEM] * 6,
        out_specs=(SMEM, SMEM, SMEM),
        cost_estimate=pl.CostEstimate(flops=10**7, bytes_accessed=10**7, transcendentals=0),
        name="plan",
    )(info, first, mask, count, blocks, rank)


def select_kernel(count, blocks, factors, picked, sems):
    def copy(i, s, n):
        return pltpu.make_async_copy(
            factors.at[i, :, pl.ds(pl.multiple_of(blocks[s, i] * BLK, BLK), BLK)], picked.at[n], sems.at[n]
        )

    def each(act):
        def left(i, n):
            def slot(s, n):
                act(copy(i, s, n))
                return n + 1

            return lax.fori_loop(0, count[i], slot, n)

        lax.fori_loop(0, NOCC, left, jnp.int32(0))

    each(lambda c: c.start())
    each(lambda c: c.wait())


def select(count, blocks, factors, room):
    rows = factors.shape[1]
    return pl.pallas_call(
        select_kernel,
        out_shape=jax.ShapeDtypeStruct((room, rows, BLK), factors.dtype),
        in_specs=[SMEM, SMEM, ANY],
        out_specs=VMEM,
        scratch_shapes=[pltpu.SemaphoreType.DMA((room,))],
        compiler_params=pltpu.CompilerParams(vmem_limit_bytes=8 * 2**20),
        name="select",
    )(count, blocks, factors)


def gather(own, beside, early):
    swap = [(0, 1), (1, 0)]
    around = [(RING * c + z, RING * c + (z + 1 - 2 * c) % RING) for c in range(2) for z in range(RING)]
    twin = lax.ppermute(own, "core", swap)
    near = lax.ppermute(own, SHARE, around)
    near_twin = lax.ppermute(twin, SHARE, around)
    near, extra = lax.optimization_barrier((near, beside(twin)))
    far = lax.ppermute(near, SHARE, around)
    pieces = [own, twin, near, lax.ppermute(near, "core", swap), near_twin]
    gate = lax.ppermute(near_twin[:1], "core", swap)
    done = early(pieces, extra, gate)
    far, done = lax.optimization_barrier((far, done))
    return pieces, [lax.ppermute(near_twin, "core", swap), far, lax.ppermute(far, "core", swap)], extra, done


def place(axis):
    core, at = lax.axis_index("core"), lax.axis_index(axis)
    high, mixed = at >> 1, (at >> 1) ^ (at & 1)
    return jnp.where(core == 0, mixed, high), jnp.where(core == 0, high, mixed)


def exchange(values, axis, second):
    axes = tuple(name for name in AXES if name in ("core", axis))
    number = (lambda core, at: 2 * at + core) if axis == "x" else (lambda core, at: RING * core + at)
    pairs = []
    for core in range(2):
        for at in range(RING):
            other = at ^ 1 if core == second else RING - 1 - at
            pairs.append((number(core, at), number(core, other)))
    return lax.ppermute(values, axes, pairs)


def add(*terms):
    return functools.reduce(jnp.add, [t.astype(jnp.float32) for t in terms])


def sum_flow(keep, send, axes):
    first, last = axes
    come = [exchange(send, first, 0)]
    for axis, second in ((first, 1), (last, 0), (last, 1)):
        terms = [keep] + come
        terms = [t[(0,) * (t.ndim - come[-1].ndim)][1] for t in terms]
        come.append(exchange(add(*terms).astype(keep.dtype), axis, second))
    return add(*[t[(0,) * (t.ndim - 3)] for t in [keep] + come])


def product_kernel(flow, count, based, gates, steps, where, mine, *refs):
    slabs, refs = refs[:count], refs[count:]
    base, outs, left = refs[:based], refs[based + gates : -1], refs[-1]
    pairs = steps[0]
    last = flow is not None

    def block(n):
        return jnp.concatenate([slab[n] for slab in slabs], axis=0)

    def run(flow, _):
        begin = 2 * flow * pairs
        rows, parity = mine[2 * flow], mine[2 * flow + 1]

        def turn(n, _):
            turned = block(n).T
            for g in range(BLK // PART):
                left[n, g ^ rows] = turned[g * PART : (g + 1) * PART]
            return 0

        def some(m, _):
            for n in range(UNROLL):
                u = jnp.minimum(UNROLL * m + n, pairs - 1)
                for k in range(2):
                    code = where[begin + 2 * u + (k ^ parity)]
                    lhs = left[code & 255].reshape(BLK, -1)
                    full = jnp.dot(lhs, block((code >> 8) & 255), preferred_element_type=jnp.float32)
                    if based:
                        full += base[0][flow, u, k]
                    if last:
                        full = full.reshape(2, 2, 2, PART, BLK).astype(jnp.bfloat16)
                        outs[0][:, :, k, u] = full[0]
                        outs[1][:, :, k, u] = full[1]
                    else:
                        outs[0][flow, u, k] = full
            return 0

        low = (where[begin] >> 16) & 255
        high = where[begin + 2 * pairs - 1] >> 24
        lax.fori_loop(low, high + 1, turn, 0)
        lax.fori_loop(0, (pairs + UNROLL - 1) // UNROLL, some, 0)
        return 0

    @pl.when(pairs > 0)
    def _():
        if last:
            run(flow, 0)
        else:
            lax.fori_loop(0, 2, run, 0)


def products(flow, steps, where, mine, slabs, room, base=None, gate=()):
    blocks, rows, _ = slabs[0].shape
    pairs = room // 4
    whole = jax.ShapeDtypeStruct((2, pairs, 2, BLK, BLK), jnp.float32)
    half = jax.ShapeDtypeStruct((2, 2, 2, pairs, PART, BLK), jnp.bfloat16)
    extra = [] if base is None else [base]
    depth = len(slabs) * rows
    need = 2 * 2 * blocks * depth * BLK + 4 * pairs * BLK * BLK * (6 if extra else 1 if flow is not None else 4) + 4 * 2**20
    return pl.pallas_call(
        functools.partial(product_kernel, flow, len(slabs), len(extra), len(gate)),
        out_shape=whole if flow is None else (half, half),
        in_specs=[SMEM] * 3 + [VMEM] * (len(slabs) + len(extra)) + [ANY] * len(gate),
        out_specs=VMEM if flow is None else (VMEM, VMEM),
        scratch_shapes=[pltpu.VMEM((blocks, BLK // PART, PART, depth), jnp.bfloat16)],
        compiler_params=pltpu.CompilerParams(vmem_limit_bytes=need),
        cost_estimate=pl.CostEstimate(flops=10**4, bytes_accessed=10**4, transcendentals=0),
        name="products",
    )(steps, where, mine, *slabs, *extra, *gate)


def energy_kernel(steps, what, mine, partners, pair_count, eps_occ, *refs):
    sums, eps_rows, (eps_lanes, out, acc, lines) = refs[:2], refs[2:4], refs[4:]
    acc[...] = jnp.zeros_like(acc)
    pairs = steps[0]

    def step(u, _):
        for flow in range(2):
            code = what[2 * (flow * pairs + u) + mine[2 * flow + 1]]
            pair = code & 511
            real = jnp.minimum(pair, NONE - 1)
            i, j = real // NOCC, real % NOCC
            value = sums[flow][u]
            bottom = eps_rows[flow][(code >> 9) & 31] + eps_lanes[pl.ds(code >> 14, 1), :] - eps_occ[i] - eps_occ[j]
            term = value * value / bottom
            acc[pair] += term[: PART // 2] + term[PART // 2 :]
        return 0

    lax.fori_loop(0, pairs, step, 0)

    def line(i, _):
        lanes = []
        for p in range(NPAIR):
            j = partners[p, i]
            pair = jnp.where(p < pair_count[i], jnp.minimum(i, j) * NOCC + jnp.maximum(i, j), NONE + 1)
            lanes.append(jnp.sum(acc[pair], axis=0, keepdims=True))
        lines[i] = jnp.concatenate(lanes, axis=0)
        return 0

    lax.fori_loop(0, NOCC, line, 0)
    table = -jnp.sum(lines[...], axis=2)
    out[...] = jnp.concatenate([table, jnp.zeros((NOCC, BLK - NPAIR), jnp.float32)], axis=1)


def energies(steps, what, mine, partners, pair_count, eps_occ, sums, eps_rows, eps_lanes):
    return pl.pallas_call(
        energy_kernel,
        out_shape=jax.ShapeDtypeStruct((NOCC, BLK), jnp.float32),
        in_specs=[SMEM] * 6 + [VMEM] * 5,
        out_specs=VMEM,
        scratch_shapes=[
            pltpu.VMEM((NONE + 8, PART // 2, BLK), jnp.float32),
            pltpu.VMEM((NOCC, NPAIR, BLK), jnp.float32),
        ],
        compiler_params=pltpu.CompilerParams(vmem_limit_bytes=8 * sums[0].size + 6 * 2**20),
        name="energies",
    )(steps, what, mine, partners, pair_count, eps_occ, *sums, *eps_rows, eps_lanes)


def body(b_factors, eps_occ, eps_virt, dom_blocks, dom_count, partners, pair_count):
    blocks, partners = dom_blocks.T, partners.T
    rank = lax.axis_index(SHARE).astype(jnp.int32).reshape(1)
    info, first, mask = make_sizes(dom_count, partners, pair_count)

    first_x, second_x = place("x")
    first_y, second_y = place("y")
    rows = (4 * first_x + 2 * second_x + first_y, 4 * first_y + 2 * second_y + first_x)
    mine = jnp.stack([rows[0], second_y, rows[1], second_x]).astype(jnp.int32)
    eps_lanes = eps_virt.reshape(-1, BLK)

    def branch(sizes):
        blocks_room, tiles_room = sizes
        split = tiles_room < 256

        def beside(twin):
            info_then, _ = lax.optimization_barrier((info, twin))
            plan = make_plan(info_then, first, mask, dom_count, blocks, rank)
            eps_rows = [lax.dynamic_slice_in_dim(eps_lanes, r * PART, PART, axis=1) for r in rows]
            return plan, [jnp.broadcast_to(e[:, :, None], e.shape + (BLK,)) for e in eps_rows]

        def early(pieces, extra, gate):
            (steps, where, _), _ = extra
            return products(None, steps, where, mine, pieces, tiles_room, gate=[gate]) if split else None

        own = select(dom_count, blocks, b_factors, blocks_room)
        pieces, late, ((steps, where, what), eps_rows), done = gather(own, beside, early)
        late = late if split else pieces + late
        sums = []
        for flow, axes in enumerate((("x", "y"), ("y", "x"))):
            keep, send = products(flow, steps, where, mine, late, tiles_room, base=done)
            sums.append(sum_flow(keep, send, axes))
        return energies(steps, what, mine, partners, pair_count, eps_occ, sums, eps_rows, eps_lanes)

    table = lax.switch(info[0], [functools.partial(branch, sizes) for sizes in SIZES])
    device_total = 128
    spread = jnp.broadcast_to(table[None], (device_total // NOCC, NOCC, BLK)).reshape(device_total, BLK)
    came = lax.all_to_all(spread, AXES, split_axis=0, concat_axis=0, tiled=True)
    return jnp.sum(came, axis=0, keepdims=True)[:, :NPAIR]


def solution(mesh):
    fine = Mesh(mesh.devices.reshape(4, 2, 4, 4), AXES)
    return jax.shard_map(
        body,
        mesh=fine,
        in_specs=(P(None, AXES, None), P(), P(), P(), P(), P(), P()),
        out_specs=P(("y", "z"), None),
        check_vma=False,
    )
```

```python
import functools

import jax
import jax.numpy as jnp
from jax import lax
from jax.experimental import pallas as pl
from jax.experimental.pallas import tpu as pltpu
from jax.sharding import Mesh
from jax.sharding import PartitionSpec as P

BLK = 128
MAXDOM = 6
NPAIR = 8
NOCC = 16
AXES = ("x", "core", "y", "z")
SHARE = ("core", "z")
NSHARE = 8
RING = 4
NSUM = 16
PART = 2 * BLK // NSUM
SIZES = ((53, 76), (59, 98), (65, 122), (73, 172), (96, 576))
MAXTILE = SIZES[-1][1]
UNROLL = 4
NONE = NOCC * NOCC

SMEM = pl.BlockSpec(memory_space=pltpu.SMEM)
VMEM = pl.BlockSpec(memory_space=pltpu.VMEM)
ANY = pl.BlockSpec(memory_space=pl.ANY)


def sizes_kernel(count, partners, pair_count, info, first, mask):
    live_blocks = jnp.int32(0)
    for i in range(NOCC):
        first[i] = live_blocks
        mask[i] = 0
        live_blocks = live_blocks + count[i]

    for i in range(NOCC):
        for p in range(NPAIR):

            @pl.when(p < pair_count[i])
            def _(i=i, p=p):
                j = partners[p, i]
                low, high = jnp.minimum(i, j), jnp.maximum(i, j)
                mask[low] = mask[low] | (jnp.int32(1) << high)

    tiles = jnp.int32(0)
    for i in range(NOCC):
        row = mask[i]
        width = jnp.int32(0)
        for j in range(i, NOCC):
            width = width + ((row >> j) & 1) * count[j]
        tiles = tiles + width * count[i]
    quota = 2 * ((tiles + 2 * NSHARE - 1) // (2 * NSHARE))
    branch = jnp.int32(len(SIZES) - 1)
    for n in reversed(range(len(SIZES) - 1)):
        fits = (live_blocks <= SIZES[n][0]) & (quota <= SIZES[n][1])
        branch = jnp.where(fits, n, branch)
    info[0] = branch
    info[1] = quota
    info[2] = tiles


def make_sizes(count, partners, pair_count):
    return pl.pallas_call(
        sizes_kernel,
        out_shape=(
            jax.ShapeDtypeStruct((4,), jnp.int32),
            jax.ShapeDtypeStruct((NOCC,), jnp.int32),
            jax.ShapeDtypeStruct((NOCC,), jnp.int32),
        ),
        in_specs=[SMEM] * 3,
        out_specs=(SMEM, SMEM, SMEM),
        name="sizes",
    )(count, partners, pair_count)


def late_share(pairs):
    return 7 * pairs // 16


def plan_kernel(info, first, mask, count, blocks, rank, mine, steps, where, what):
    low_tile = rank[0] * info[1]
    high_tile = jnp.minimum(low_tile + info[1], info[2])

    def left(i, start):
        def right(j, start):
            width = count[j]
            size = jnp.where(((mask[i] >> j) & 1) == 1, count[i] * width, 0)

            @pl.when((start < high_tile) & (start + size > low_tile))
            def _():
                span = (first[i] << 16) | ((first[i] + count[i] - 1) << 24)

                def row(s, begin):
                    lo = jnp.maximum(low_tile - begin, 0)
                    hi = jnp.minimum(high_tile - begin, width)

                    def tile(t, _):
                        n = begin + t - low_tile
                        where[n] = (first[i] + s) | ((first[j] + t) << 8) | span
                        what[n] = (i * NOCC + j) | (blocks[s, i] << 9) | (blocks[t, j] << 14)
                        return 0

                    lax.fori_loop(lo, hi, tile, 0)
                    return begin + width

                lax.fori_loop(0, count[i], row, start)

            return start + size

        return lax.fori_loop(i, NOCC, right, start)

    lax.fori_loop(0, NOCC, left, jnp.int32(0))
    tiles = jnp.maximum(high_tile - low_tile, 0)

    pairs = (tiles + 1) // 2

    @pl.when(tiles % 2 == 1)
    def _():
        where[tiles] = where[tiles - 1]
        what[tiles] = NONE

    steps[0] = late_share(pairs)
    steps[1] = pairs - late_share(pairs)
    for n in range(5):
        steps[2 + n] = mine[n]


def make_plan(info, first, mask, count, blocks, rank, mine):
    return pl.pallas_call(
        plan_kernel,
        out_shape=(
            jax.ShapeDtypeStruct((7,), jnp.int32),
            jax.ShapeDtypeStruct((MAXTILE,), jnp.int32),
            jax.ShapeDtypeStruct((MAXTILE,), jnp.int32),
        ),
        in_specs=[SMEM] * 7,
        out_specs=(SMEM, SMEM, SMEM),
        cost_estimate=pl.CostEstimate(flops=10**7, bytes_accessed=10**7, transcendentals=0),
        name="plan",
    )(info, first, mask, count, blocks, rank, mine)


def select_kernel(count, blocks, factors, picked, sem):
    def left(i, live):
        for s in range(MAXDOM):

            @pl.when(s < count[i])
            def _(s=s):
                column = pl.multiple_of(blocks[s, i] * BLK, BLK)
                pltpu.make_async_copy(factors.at[i, :, pl.ds(column, BLK)], picked.at[live + s], sem).start()

        return live + count[i]

    live = lax.fori_loop(0, NOCC, left, jnp.int32(0))
    room = picked.shape[0]
    for bit in range(room.bit_length()):

        @pl.when((live >> bit) & 1 == 1)
        def _(bit=bit):
            some = picked.at[pl.ds(0, 1 << bit)]
            pltpu.make_async_copy(some, some, sem).wait()


def select(count, blocks, factors, room):
    rows = factors.shape[1]
    return pl.pallas_call(
        select_kernel,
        out_shape=jax.ShapeDtypeStruct((room, rows, BLK), factors.dtype),
        in_specs=[SMEM, SMEM, ANY],
        out_specs=VMEM,
        scratch_shapes=[pltpu.SemaphoreType.DMA],
        compiler_params=pltpu.CompilerParams(vmem_limit_bytes=8 * 2**20),
        name="select",
    )(count, blocks, factors)


def gather(own, beside, early):
    swap = [(0, 1), (1, 0)]
    around = [(RING * c + z, RING * c + (z + 1 - 2 * c) % RING) for c in range(2) for z in range(RING)]
    twin = lax.ppermute(own, "core", swap)
    near = lax.ppermute(own, SHARE, around)
    near_twin = lax.ppermute(twin, SHARE, around)
    near, extra = lax.optimization_barrier((near, beside(twin)))
    far = lax.ppermute(near, SHARE, around)
    pieces = [own, twin, near, lax.ppermute(near, "core", swap), near_twin]
    gate = lax.ppermute(near_twin[:1], "core", swap)
    done = early(pieces, extra, gate)
    far, done = lax.optimization_barrier((far, done))
    return pieces, [lax.ppermute(near_twin, "core", swap), far, lax.ppermute(far, "core", swap)], extra, done


def place(axis):
    core, at = lax.axis_index("core"), lax.axis_index(axis)
    high, mixed = at >> 1, (at >> 1) ^ (at & 1)
    return jnp.where(core == 0, mixed, high), jnp.where(core == 0, high, mixed)


def exchange(values, axis, second):
    axes = tuple(name for name in AXES if name in ("core", axis))
    number = (lambda core, at: 2 * at + core) if axis == "x" else (lambda core, at: RING * core + at)
    pairs = []
    for core in range(2):
        for at in range(RING):
            other = at ^ 1 if core == second else RING - 1 - at
            pairs.append((number(core, at), number(core, other)))
    return lax.ppermute(values, axes, pairs)


def add(*terms):
    return functools.reduce(jnp.add, [t.astype(jnp.float32) for t in terms])


def sum_flow(keep, send, axes):
    first, last = axes
    come = [exchange(send, first, 0)]
    for axis, second in ((first, 1), (last, 0), (last, 1)):
        terms = [keep] + come
        terms = [t[(0,) * (t.ndim - come[-1].ndim)][1] for t in terms]
        come.append(exchange(add(*terms).astype(keep.dtype), axis, second))
    return add(*[t[(0,) * (t.ndim - 3)] for t in [keep] + come])


def product_kernel(flow, count, based, gates, direct, steps, where, *refs):
    slabs, refs = refs[:count], refs[count:]
    base, outs, left = refs[:based], refs[based + gates : -1], refs[-1]
    last = flow is not None

    def block(n):
        return jnp.concatenate([slab[n] for slab in slabs], axis=0)

    def run(flow, _):
        begin, pairs = flow * steps[0], steps[flow]
        rows, parity = (0, 0) if direct else (steps[2 + 2 * flow], steps[3 + 2 * flow])

        def turn(n, _):
            turned = block(n).T
            for g in range(BLK // PART):
                left[n, g ^ rows] = turned[g * PART : (g + 1) * PART]
            return 0

        def some(m, _):
            for n in range(UNROLL):
                u = jnp.minimum(UNROLL * m + n, pairs - 1)
                for k in range(2):
                    code = where[2 * (begin + u) + (k ^ parity)]
                    lhs = left[code & 255].reshape(BLK, -1)
                    full = jnp.dot(lhs, block((code >> 8) & 255), preferred_element_type=jnp.float32)
                    if based:
                        full += base[0][begin + u, k]
                    if direct:
                        parts = full.reshape(BLK // PART, PART, BLK).astype(jnp.bfloat16)
                        for g in range(BLK // PART):
                            outs[0][owner(flow, 2 * g + k, steps[6]), u] = parts[g]
                    elif last:
                        full = full.reshape(2, 2, 2, PART, BLK).astype(jnp.bfloat16)
                        outs[0][:, :, k, u] = full[0]
                        outs[1][:, :, k, u] = full[1]
                    else:
                        outs[0][begin + u, k] = full
            return 0

        @pl.when(pairs > 0)
        def _():
            low = (where[2 * begin] >> 16) & 255
            high = where[2 * (begin + pairs) - 1] >> 24
            lax.fori_loop(low, high + 1, turn, 0)
            lax.fori_loop(0, (pairs + UNROLL - 1) // UNROLL, some, 0)

        return 0

    if last:
        run(flow, 0)
    else:
        lax.fori_loop(0, 2, run, 0)


def owner(flow, part, core):
    at = []
    for first, second in ((part >> 3 & 1, part >> 2 & 1), (part >> 1 & 1, part & 1)):
        at.append(2 * jnp.where(core == 0, second, first) + (first ^ second))
    return RING * at[flow] + at[1 - flow]


def products(flow, steps, where, slabs, room, base=None, gate=(), direct=False):
    blocks, rows, _ = slabs[0].shape
    pairs = room // 2
    whole = jax.ShapeDtypeStruct((pairs, 2, BLK, BLK), jnp.float32)
    part = pairs if flow is None else pairs - late_share(pairs) if flow else late_share(pairs)
    half = jax.ShapeDtypeStruct((2, 2, 2, part, PART, BLK), jnp.bfloat16)
    spread = jax.ShapeDtypeStruct((NSUM, part, PART, BLK), jnp.bfloat16)
    extra = [] if base is None else [base]
    depth = len(slabs) * rows
    need = 2 * 2 * blocks * depth * BLK + 2 * pairs * BLK * BLK * (6 if extra else 2 if flow is not None else 4) + 4 * 2**20
    return pl.pallas_call(
        functools.partial(product_kernel, flow, len(slabs), len(extra), len(gate), direct),
        out_shape=whole if flow is None else spread if direct else (half, half),
        in_specs=[SMEM] * 2 + [VMEM] * (len(slabs) + len(extra)) + [ANY] * len(gate),
        out_specs=VMEM if flow is None or direct else (VMEM, VMEM),
        scratch_shapes=[pltpu.VMEM((blocks, BLK // PART, PART, depth), jnp.bfloat16)],
        compiler_params=pltpu.CompilerParams(vmem_limit_bytes=need),
        cost_estimate=pl.CostEstimate(flops=10**4, bytes_accessed=10**4, transcendentals=0),
        name="products",
    )(steps, where, *slabs, *extra, *gate)


def energy_kernel(steps, what, partners, pair_count, eps_occ, *refs):
    sums, eps_rows, (eps_lanes, out, acc, lines) = refs[:2], refs[2:4], refs[4:]
    acc[...] = jnp.zeros_like(acc)
    for flow in range(2):

        def step(u, _, flow=flow):
            code = what[2 * (flow * steps[0] + u) + steps[3 + 2 * flow]]
            pair = code & 511
            real = jnp.minimum(pair, NONE - 1)
            i, j = real // NOCC, real % NOCC
            value = sums[flow][u]
            bottom = eps_rows[flow][(code >> 9) & 31] + eps_lanes[pl.ds(code >> 14, 1), :] - eps_occ[i] - eps_occ[j]
            term = value * value / bottom
            acc[pair] += term[: PART // 2] + term[PART // 2 :]
            return 0

        lax.fori_loop(0, steps[flow], step, 0)

    def line(i, _):
        lanes = []
        for p in range(NPAIR):
            j = partners[p, i]
            pair = jnp.where(p < pair_count[i], jnp.minimum(i, j) * NOCC + jnp.maximum(i, j), NONE + 1)
            lanes.append(jnp.sum(acc[pair], axis=0, keepdims=True))
        lines[i] = jnp.concatenate(lanes, axis=0)
        return 0

    lax.fori_loop(0, NOCC, line, 0)
    table = -jnp.sum(lines[...], axis=2)
    out[...] = jnp.concatenate([table, jnp.zeros((NOCC, BLK - NPAIR), jnp.float32)], axis=1)


def energies(steps, what, partners, pair_count, eps_occ, sums, eps_rows, eps_lanes):
    return pl.pallas_call(
        energy_kernel,
        out_shape=jax.ShapeDtypeStruct((NOCC, BLK), jnp.float32),
        in_specs=[SMEM] * 5 + [VMEM] * 5,
        out_specs=VMEM,
        scratch_shapes=[
            pltpu.VMEM((NONE + 8, PART // 2, BLK), jnp.float32),
            pltpu.VMEM((NOCC, NPAIR, BLK), jnp.float32),
        ],
        compiler_params=pltpu.CompilerParams(vmem_limit_bytes=8 * sums[0].size + 6 * 2**20),
        name="energies",
    )(steps, what, partners, pair_count, eps_occ, *sums, *eps_rows, eps_lanes)


def sum_any(spread):
    come = lax.all_to_all(spread, ("x", "y"), split_axis=0, concat_axis=0, tiled=True)
    return jnp.sum(come.astype(jnp.float32), axis=0)


def body(b_factors, eps_occ, eps_virt, dom_blocks, dom_count, partners, pair_count):
    blocks, partners = dom_blocks.T, partners.T
    rank = lax.axis_index(SHARE).astype(jnp.int32).reshape(1)
    info, first, mask = make_sizes(dom_count, partners, pair_count)

    first_x, second_x = place("x")
    first_y, second_y = place("y")
    rows = (4 * first_x + 2 * second_x + first_y, 4 * first_y + 2 * second_y + first_x)
    mine = jnp.stack([rows[0], second_y, rows[1], second_x, lax.axis_index("core")]).astype(jnp.int32)
    eps_lanes = eps_virt.reshape(-1, BLK)

    def branch(sizes):
        blocks_room, tiles_room = sizes
        split = tiles_room < MAXTILE

        def beside(twin):
            info_then, _ = lax.optimization_barrier((info, twin))
            plan = make_plan(info_then, first, mask, dom_count, blocks, rank, mine)
            eps_rows = [lax.dynamic_slice_in_dim(eps_lanes, r * PART, PART, axis=1) for r in rows]
            return plan, [jnp.broadcast_to(e[:, :, None], e.shape + (BLK,)) for e in eps_rows]

        def early(pieces, extra, gate):
            (steps, where, _), _ = extra
            return products(None, steps, where, pieces, tiles_room, gate=[gate])

        own = select(dom_count, blocks, b_factors, blocks_room)
        if split:
            _, late, ((steps, where, what), eps_rows), done = gather(own, beside, early)
        else:
            (steps, where, what), eps_rows = beside(own)
            copies = jnp.broadcast_to(own[None], (NSHARE,) + own.shape)
            slabs = lax.all_to_all(copies, SHARE, split_axis=0, concat_axis=0, tiled=True)
            late = [slabs[n] for n in range(NSHARE)]
        sums = []
        for flow, axes in enumerate((("x", "y"), ("y", "x"))):
            if split:
                keep, send = products(flow, steps, where, late, tiles_room, base=done)
                sums.append(sum_flow(keep, send, axes))
            else:
                sums.append(sum_any(products(flow, steps, where, late, tiles_room, direct=True)))
        return energies(steps, what, partners, pair_count, eps_occ, sums, eps_rows, eps_lanes)

    table = lax.switch(info[0], [functools.partial(branch, sizes) for sizes in SIZES])
    device_total = 128
    spread = jnp.broadcast_to(table[None], (device_total // NOCC, NOCC, BLK)).reshape(device_total, BLK)
    came = lax.all_to_all(spread, AXES, split_axis=0, concat_axis=0, tiled=True)
    return jnp.sum(came, axis=0, keepdims=True)[:, :NPAIR]


def solution(mesh):
    fine = Mesh(mesh.devices.reshape(4, 2, 4, 4), AXES)
    return jax.shard_map(
        body,
        mesh=fine,
        in_specs=(P(None, AXES, None), P(), P(), P(), P(), P(), P()),
        out_specs=P(("y", "z"), None),
        check_vma=False,
    )
```

```python
import functools

import jax
import jax.numpy as jnp
from jax import lax
from jax.experimental import pallas as pl
from jax.experimental.pallas import tpu as pltpu
from jax.sharding import Mesh
from jax.sharding import PartitionSpec as P

BLK = 128
MAXDOM = 6
NPAIR = 8
NOCC = 16
AXES = ("x", "core", "y", "z")
SHARE = ("core", "z")
NSHARE = 8
RING = 4
NSUM = 16
PART = 2 * BLK // NSUM
SIZES = ((58, 90), (65, 122), (73, 172), (96, 576))
MAXTILE = SIZES[-1][1]
UNROLL = 4
NONE = NOCC * NOCC

SMEM = pl.BlockSpec(memory_space=pltpu.SMEM)
VMEM = pl.BlockSpec(memory_space=pltpu.VMEM)
ANY = pl.BlockSpec(memory_space=pl.ANY)


def sizes_kernel(count, partners, pair_count, info, first, mask):
    live_blocks = jnp.int32(0)
    for i in range(NOCC):
        first[i] = live_blocks
        mask[i] = 0
        live_blocks = live_blocks + count[i]

    for i in range(NOCC):
        for p in range(NPAIR):

            @pl.when(p < pair_count[i])
            def _(i=i, p=p):
                j = partners[p, i]
                low, high = jnp.minimum(i, j), jnp.maximum(i, j)
                mask[low] = mask[low] | (jnp.int32(1) << high)

    tiles = jnp.int32(0)
    for i in range(NOCC):
        row = mask[i]
        width = jnp.int32(0)
        for j in range(i, NOCC):
            width = width + ((row >> j) & 1) * count[j]
        tiles = tiles + width * count[i]
    quota = 2 * ((tiles + 2 * NSHARE - 1) // (2 * NSHARE))
    branch = jnp.int32(len(SIZES) - 1)
    for n in reversed(range(len(SIZES) - 1)):
        fits = (live_blocks <= SIZES[n][0]) & (quota <= SIZES[n][1])
        branch = jnp.where(fits, n, branch)
    info[0] = branch
    info[1] = quota
    info[2] = tiles


def make_sizes(count, partners, pair_count):
    return pl.pallas_call(
        sizes_kernel,
        out_shape=(
            jax.ShapeDtypeStruct((4,), jnp.int32),
            jax.ShapeDtypeStruct((NOCC,), jnp.int32),
            jax.ShapeDtypeStruct((NOCC,), jnp.int32),
        ),
        in_specs=[SMEM] * 3,
        out_specs=(SMEM, SMEM, SMEM),
        name="sizes",
    )(count, partners, pair_count)


def late_share(pairs):
    return 7 * pairs // 16


def plan_kernel(info, first, mask, count, blocks, rank, mine, steps, where, what):
    low_tile = rank[0] * info[1]
    high_tile = jnp.minimum(low_tile + info[1], info[2])

    def left(i, start):
        def right(j, start):
            width = count[j]
            size = jnp.where(((mask[i] >> j) & 1) == 1, count[i] * width, 0)

            @pl.when((start < high_tile) & (start + size > low_tile))
            def _():
                span = (first[i] << 16) | ((first[i] + count[i] - 1) << 24)

                def row(s, begin):
                    lo = jnp.maximum(low_tile - begin, 0)
                    hi = jnp.minimum(high_tile - begin, width)

                    def tile(t, _):
                        n = begin + t - low_tile
                        where[n] = (first[i] + s) | ((first[j] + t) << 8) | span
                        what[n] = (i * NOCC + j) | (blocks[s, i] << 9) | (blocks[t, j] << 14)
                        return 0

                    lax.fori_loop(lo, hi, tile, 0)
                    return begin + width

                lax.fori_loop(0, count[i], row, start)

            return start + size

        return lax.fori_loop(i, NOCC, right, start)

    lax.fori_loop(0, NOCC, left, jnp.int32(0))
    tiles = jnp.maximum(high_tile - low_tile, 0)

    pairs = (tiles + 1) // 2

    @pl.when(tiles % 2 == 1)
    def _():
        where[tiles] = where[tiles - 1]
        what[tiles] = NONE

    steps[0] = late_share(pairs)
    steps[1] = pairs - late_share(pairs)
    for n in range(4):
        steps[2 + n] = mine[n]


def make_plan(info, first, mask, count, blocks, rank, mine):
    return pl.pallas_call(
        plan_kernel,
        out_shape=(
            jax.ShapeDtypeStruct((6,), jnp.int32),
            jax.ShapeDtypeStruct((MAXTILE,), jnp.int32),
            jax.ShapeDtypeStruct((MAXTILE,), jnp.int32),
        ),
        in_specs=[SMEM] * 7,
        out_specs=(SMEM, SMEM, SMEM),
        cost_estimate=pl.CostEstimate(flops=10**7, bytes_accessed=10**7, transcendentals=0),
        name="plan",
    )(info, first, mask, count, blocks, rank, mine)


def select_kernel(count, blocks, factors, picked, sem):
    def left(i, live):
        for s in range(MAXDOM):

            @pl.when(s < count[i])
            def _(s=s):
                column = pl.multiple_of(blocks[s, i] * BLK, BLK)
                pltpu.make_async_copy(factors.at[i, :, pl.ds(column, BLK)], picked.at[live + s], sem).start()

        return live + count[i]

    live = lax.fori_loop(0, NOCC, left, jnp.int32(0))
    room = picked.shape[0]
    for bit in range(room.bit_length()):

        @pl.when((live >> bit) & 1 == 1)
        def _(bit=bit):
            some = picked.at[pl.ds(0, 1 << bit)]
            pltpu.make_async_copy(some, some, sem).wait()


def select(count, blocks, factors, room):
    rows = factors.shape[1]
    return pl.pallas_call(
        select_kernel,
        out_shape=jax.ShapeDtypeStruct((room, rows, BLK), factors.dtype),
        in_specs=[SMEM, SMEM, ANY],
        out_specs=VMEM,
        scratch_shapes=[pltpu.SemaphoreType.DMA],
        compiler_params=pltpu.CompilerParams(vmem_limit_bytes=8 * 2**20),
        name="select",
    )(count, blocks, factors)


def gather(own, beside, early):
    swap = [(0, 1), (1, 0)]
    around = [(RING * c + z, RING * c + (z + 1 - 2 * c) % RING) for c in range(2) for z in range(RING)]
    twin = lax.ppermute(own, "core", swap)
    near = lax.ppermute(own, SHARE, around)
    near_twin = lax.ppermute(twin, SHARE, around)
    near, extra = lax.optimization_barrier((near, beside(twin)))
    far = lax.ppermute(near, SHARE, around)
    pieces = [own, twin, near, lax.ppermute(near, "core", swap), near_twin]
    gate = lax.ppermute(near_twin[:1], "core", swap)
    done = early(pieces, extra, gate)
    far, done = lax.optimization_barrier((far, done))
    return pieces, [lax.ppermute(near_twin, "core", swap), far, lax.ppermute(far, "core", swap)], extra, done


def place(axis):
    core, at = lax.axis_index("core"), lax.axis_index(axis)
    high, mixed = at >> 1, (at >> 1) ^ (at & 1)
    return jnp.where(core == 0, mixed, high), jnp.where(core == 0, high, mixed)


def exchange(values, axis, second):
    axes = tuple(name for name in AXES if name in ("core", axis))
    number = (lambda core, at: 2 * at + core) if axis == "x" else (lambda core, at: RING * core + at)
    pairs = []
    for core in range(2):
        for at in range(RING):
            other = at ^ 1 if core == second else RING - 1 - at
            pairs.append((number(core, at), number(core, other)))
    return lax.ppermute(values, axes, pairs)


def add(*terms):
    return functools.reduce(jnp.add, [t.astype(jnp.float32) for t in terms])


def sum_flow(keep, send, axes):
    first, last = axes
    come = [exchange(send, first, 0)]
    for axis, second in ((first, 1), (last, 0), (last, 1)):
        terms = [keep] + come
        terms = [t[(0,) * (t.ndim - come[-1].ndim)][1] for t in terms]
        come.append(exchange(add(*terms).astype(keep.dtype), axis, second))
    return add(*[t[(0,) * (t.ndim - 3)] for t in [keep] + come])


def product_kernel(flow, count, based, gates, steps, where, *refs):
    slabs, refs = refs[:count], refs[count:]
    base, outs, left = refs[:based], refs[based + gates : -1], refs[-1]
    last = flow is not None

    def block(n):
        return jnp.concatenate([slab[n] for slab in slabs], axis=0)

    def run(flow, _):
        begin, pairs = flow * steps[0], steps[flow]
        rows, parity = steps[2 + 2 * flow], steps[3 + 2 * flow]

        def turn(n, _):
            turned = block(n).T
            for g in range(BLK // PART):
                left[n, g ^ rows] = turned[g * PART : (g + 1) * PART]
            return 0

        def some(m, _):
            for n in range(UNROLL):
                u = jnp.minimum(UNROLL * m + n, pairs - 1)
                for k in range(2):
                    code = where[2 * (begin + u) + (k ^ parity)]
                    lhs = left[code & 255].reshape(BLK, -1)
                    full = jnp.dot(lhs, block((code >> 8) & 255), preferred_element_type=jnp.float32)
                    if based:
                        full += base[0][begin + u, k]
                    if last:
                        full = full.reshape(2, 2, 2, PART, BLK).astype(jnp.bfloat16)
                        outs[0][:, :, k, u] = full[0]
                        outs[1][:, :, k, u] = full[1]
                    else:
                        outs[0][begin + u, k] = full
            return 0

        @pl.when(pairs > 0)
        def _():
            low = (where[2 * begin] >> 16) & 255
            high = where[2 * (begin + pairs) - 1] >> 24
            lax.fori_loop(low, high + 1, turn, 0)
            lax.fori_loop(0, (pairs + UNROLL - 1) // UNROLL, some, 0)

        return 0

    if last:
        run(flow, 0)
    else:
        lax.fori_loop(0, 2, run, 0)


def products(flow, steps, where, slabs, room, base=None, gate=()):
    blocks, rows, _ = slabs[0].shape
    pairs = room // 2
    whole = jax.ShapeDtypeStruct((pairs, 2, BLK, BLK), jnp.float32)
    part = pairs if flow is None else pairs - late_share(pairs) if flow else late_share(pairs)
    half = jax.ShapeDtypeStruct((2, 2, 2, part, PART, BLK), jnp.bfloat16)
    extra = [] if base is None else [base]
    depth = len(slabs) * rows
    need = 2 * 2 * blocks * depth * BLK + 2 * pairs * BLK * BLK * (6 if extra else 2 if flow is not None else 4) + 4 * 2**20
    return pl.pallas_call(
        functools.partial(product_kernel, flow, len(slabs), len(extra), len(gate)),
        out_shape=whole if flow is None else (half, half),
        in_specs=[SMEM] * 2 + [VMEM] * (len(slabs) + len(extra)) + [ANY] * len(gate),
        out_specs=VMEM if flow is None else (VMEM, VMEM),
        scratch_shapes=[pltpu.VMEM((blocks, BLK // PART, PART, depth), jnp.bfloat16)],
        compiler_params=pltpu.CompilerParams(vmem_limit_bytes=need),
        cost_estimate=pl.CostEstimate(flops=10**4, bytes_accessed=10**4, transcendentals=0),
        name="products",
    )(steps, where, *slabs, *extra, *gate)


def energy_kernel(steps, what, partners, pair_count, eps_occ, *refs):
    sums, eps_rows, (eps_lanes, out, acc, lines) = refs[:2], refs[2:4], refs[4:]
    acc[...] = jnp.zeros_like(acc)
    for flow in range(2):

        def step(u, _, flow=flow):
            code = what[2 * (flow * steps[0] + u) + steps[3 + 2 * flow]]
            pair = code & 511
            real = jnp.minimum(pair, NONE - 1)
            i, j = real // NOCC, real % NOCC
            value = sums[flow][u]
            bottom = eps_rows[flow][(code >> 9) & 31] + eps_lanes[pl.ds(code >> 14, 1), :] - eps_occ[i] - eps_occ[j]
            term = value * value / bottom
            acc[pair] += term[: PART // 2] + term[PART // 2 :]
            return 0

        lax.fori_loop(0, steps[flow], step, 0)

    def line(i, _):
        lanes = []
        for p in range(NPAIR):
            j = partners[p, i]
            pair = jnp.where(p < pair_count[i], jnp.minimum(i, j) * NOCC + jnp.maximum(i, j), NONE + 1)
            lanes.append(jnp.sum(acc[pair], axis=0, keepdims=True))
        lines[i] = jnp.concatenate(lanes, axis=0)
        return 0

    lax.fori_loop(0, NOCC, line, 0)
    table = -jnp.sum(lines[...], axis=2)
    out[...] = jnp.concatenate([table, jnp.zeros((NOCC, BLK - NPAIR), jnp.float32)], axis=1)


def energies(steps, what, partners, pair_count, eps_occ, sums, eps_rows, eps_lanes):
    return pl.pallas_call(
        energy_kernel,
        out_shape=jax.ShapeDtypeStruct((NOCC, BLK), jnp.float32),
        in_specs=[SMEM] * 5 + [VMEM] * 5,
        out_specs=VMEM,
        scratch_shapes=[
            pltpu.VMEM((NONE + 8, PART // 2, BLK), jnp.float32),
            pltpu.VMEM((NOCC, NPAIR, BLK), jnp.float32),
        ],
        compiler_params=pltpu.CompilerParams(vmem_limit_bytes=8 * sums[0].size + 6 * 2**20),
        name="energies",
    )(steps, what, partners, pair_count, eps_occ, *sums, *eps_rows, eps_lanes)


def body(b_factors, eps_occ, eps_virt, dom_blocks, dom_count, partners, pair_count):
    blocks, partners = dom_blocks.T, partners.T
    rank = lax.axis_index(SHARE).astype(jnp.int32).reshape(1)
    info, first, mask = make_sizes(dom_count, partners, pair_count)

    first_x, second_x = place("x")
    first_y, second_y = place("y")
    rows = (4 * first_x + 2 * second_x + first_y, 4 * first_y + 2 * second_y + first_x)
    mine = jnp.stack([rows[0], second_y, rows[1], second_x]).astype(jnp.int32)
    eps_lanes = eps_virt.reshape(-1, BLK)

    def branch(sizes):
        blocks_room, tiles_room = sizes
        split = tiles_room < 256

        def beside(twin):
            info_then, _ = lax.optimization_barrier((info, twin))
            plan = make_plan(info_then, first, mask, dom_count, blocks, rank, mine)
            eps_rows = [lax.dynamic_slice_in_dim(eps_lanes, r * PART, PART, axis=1) for r in rows]
            return plan, [jnp.broadcast_to(e[:, :, None], e.shape + (BLK,)) for e in eps_rows]

        def early(pieces, extra, gate):
            (steps, where, _), _ = extra
            return products(None, steps, where, pieces, tiles_room, gate=[gate]) if split else None

        own = select(dom_count, blocks, b_factors, blocks_room)
        pieces, late, ((steps, where, what), eps_rows), done = gather(own, beside, early)
        late = late if split else pieces + late
        sums = []
        for flow, axes in enumerate((("x", "y"), ("y", "x"))):
            keep, send = products(flow, steps, where, late, tiles_room, base=done)
            sums.append(sum_flow(keep, send, axes))
        return energies(steps, what, partners, pair_count, eps_occ, sums, eps_rows, eps_lanes)

    table = lax.switch(info[0], [functools.partial(branch, sizes) for sizes in SIZES])
    device_total = 128
    spread = jnp.broadcast_to(table[None], (device_total // NOCC, NOCC, BLK)).reshape(device_total, BLK)
    came = lax.all_to_all(spread, AXES, split_axis=0, concat_axis=0, tiled=True)
    return jnp.sum(came, axis=0, keepdims=True)[:, :NPAIR]


def solution(mesh):
    fine = Mesh(mesh.devices.reshape(4, 2, 4, 4), AXES)
    return jax.shard_map(
        body,
        mesh=fine,
        in_specs=(P(None, AXES, None), P(), P(), P(), P(), P(), P()),
        out_specs=P(("y", "z"), None),
        check_vma=False,
    )
```

```python
import functools

import jax
import jax.numpy as jnp
from jax import lax
from jax.experimental import pallas as pl
from jax.experimental.pallas import tpu as pltpu
from jax.sharding import Mesh
from jax.sharding import PartitionSpec as P

BLK = 128
MAXDOM = 6
NPAIR = 8
NOCC = 16
AXES = ("x", "core", "y", "z")
SHARE = ("core", "z")
NSHARE = 8
RING = 4
FLIPS = ((0, 0), (1, 0))
COPIES = 8
NSUM = 16
PART = 2 * BLK // NSUM
SIZES = ((58, 90), (65, 122), (73, 172), (96, 576))
MAXTILE = SIZES[-1][1]
UNROLL = 4
NONE = NOCC * NOCC

SMEM = pl.BlockSpec(memory_space=pltpu.SMEM)
VMEM = pl.BlockSpec(memory_space=pltpu.VMEM)
ANY = pl.BlockSpec(memory_space=pl.ANY)


def sizes_kernel(count, partners, pair_count, info, first, mask):
    live_blocks = jnp.int32(0)
    for i in range(NOCC):
        first[i] = live_blocks
        mask[i] = 0
        live_blocks = live_blocks + count[i]

    for i in range(NOCC):
        for p in range(NPAIR):

            @pl.when(p < pair_count[i])
            def _(i=i, p=p):
                j = partners[p, i]
                low, high = jnp.minimum(i, j), jnp.maximum(i, j)
                mask[low] = mask[low] | (jnp.int32(1) << high)

    tiles = jnp.int32(0)
    for i in range(NOCC):
        row = mask[i]
        width = jnp.int32(0)
        for j in range(i, NOCC):
            width = width + ((row >> j) & 1) * count[j]
        tiles = tiles + width * count[i]
    quota = 2 * ((tiles + 2 * NSHARE - 1) // (2 * NSHARE))
    branch = jnp.int32(len(SIZES) - 1)
    for n in reversed(range(len(SIZES) - 1)):
        fits = (live_blocks <= SIZES[n][0]) & (quota <= SIZES[n][1])
        branch = jnp.where(fits, n, branch)
    info[0] = branch
    info[1] = quota
    info[2] = tiles


def make_sizes(count, partners, pair_count):
    return pl.pallas_call(
        sizes_kernel,
        out_shape=(
            jax.ShapeDtypeStruct((4,), jnp.int32),
            jax.ShapeDtypeStruct((NOCC,), jnp.int32),
            jax.ShapeDtypeStruct((NOCC,), jnp.int32),
        ),
        in_specs=[SMEM] * 3,
        out_specs=(SMEM, SMEM, SMEM),
        name="sizes",
    )(count, partners, pair_count)


def late_share(pairs):
    return 7 * pairs // 16


def plan_kernel(info, first, mask, count, blocks, rank, mine, steps, where, what):
    low_tile = rank[0] * info[1]
    high_tile = jnp.minimum(low_tile + info[1], info[2])

    def left(i, start):
        def right(j, start):
            width = count[j]
            size = jnp.where(((mask[i] >> j) & 1) == 1, count[i] * width, 0)

            @pl.when((start < high_tile) & (start + size > low_tile))
            def _():
                span = (first[i] << 16) | ((first[i] + count[i] - 1) << 24)

                def row(s, begin):
                    lo = jnp.maximum(low_tile - begin, 0)
                    hi = jnp.minimum(high_tile - begin, width)

                    def tile(t, _):
                        n = begin + t - low_tile
                        where[n] = (first[i] + s) | ((first[j] + t) << 8) | span
                        what[n] = (i * NOCC + j) | (blocks[s, i] << 9) | (blocks[t, j] << 14)
                        return 0

                    lax.fori_loop(lo, hi, tile, 0)
                    return begin + width

                lax.fori_loop(0, count[i], row, start)

            return start + size

        return lax.fori_loop(i, NOCC, right, start)

    lax.fori_loop(0, NOCC, left, jnp.int32(0))
    tiles = jnp.maximum(high_tile - low_tile, 0)

    pairs = (tiles + 1) // 2

    @pl.when(tiles % 2 == 1)
    def _():
        where[tiles] = where[tiles - 1]
        what[tiles] = NONE

    steps[0] = late_share(pairs)
    steps[1] = pairs - late_share(pairs)
    for n in range(4):
        steps[2 + n] = mine[n]


def make_plan(info, first, mask, count, blocks, rank, mine):
    return pl.pallas_call(
        plan_kernel,
        out_shape=(
            jax.ShapeDtypeStruct((6,), jnp.int32),
            jax.ShapeDtypeStruct((MAXTILE,), jnp.int32),
            jax.ShapeDtypeStruct((MAXTILE,), jnp.int32),
        ),
        in_specs=[SMEM] * 7,
        out_specs=(SMEM, SMEM, SMEM),
        cost_estimate=pl.CostEstimate(flops=10**7, bytes_accessed=10**7, transcendentals=0),
        name="plan",
    )(info, first, mask, count, blocks, rank, mine)


def select_kernel(count, blocks, factors, picked, sem):
    def left(i, live):
        for s in range(MAXDOM):

            @pl.when(s < count[i])
            def _(s=s):
                column = pl.multiple_of(blocks[s, i] * BLK, BLK)
                pltpu.make_async_copy(factors.at[i, :, pl.ds(column, BLK)], picked.at[live + s], sem).start()

        return live + count[i]

    live = lax.fori_loop(0, NOCC, left, jnp.int32(0))
    room = picked.shape[0]
    for bit in range(room.bit_length()):

        @pl.when((live >> bit) & 1 == 1)
        def _(bit=bit):
            some = picked.at[pl.ds(0, 1 << bit)]
            pltpu.make_async_copy(some, some, sem).wait()


def select(count, blocks, factors, room):
    rows = factors.shape[1]
    return pl.pallas_call(
        select_kernel,
        out_shape=jax.ShapeDtypeStruct((room, rows, BLK), factors.dtype),
        in_specs=[SMEM, SMEM, ANY],
        out_specs=VMEM,
        scratch_shapes=[pltpu.SemaphoreType.DMA],
        compiler_params=pltpu.CompilerParams(vmem_limit_bytes=8 * 2**20),
        name="select",
    )(count, blocks, factors)


def gather(own, beside, early):
    swap = [(0, 1), (1, 0)]
    around = [(RING * c + z, RING * c + (z + 1 - 2 * c) % RING) for c in range(2) for z in range(RING)]
    twin = lax.ppermute(own, "core", swap)
    near = lax.ppermute(own, SHARE, around)
    near_twin = lax.ppermute(twin, SHARE, around)
    near, extra = lax.optimization_barrier((near, beside(twin)))
    far = lax.ppermute(near, SHARE, around)
    pieces = [own, twin, near, lax.ppermute(near, "core", swap), near_twin]
    gate = lax.ppermute(near_twin[:1], "core", swap)
    done = early(pieces, extra, gate)
    far, done = lax.optimization_barrier((far, done))
    return pieces, [lax.ppermute(near_twin, "core", swap), far, lax.ppermute(far, "core", swap)], extra, done


def place(axis, flip):
    core, at = lax.axis_index("core") ^ flip, lax.axis_index(axis)
    high, mixed = at >> 1, (at >> 1) ^ (at & 1)
    return jnp.where(core == 0, mixed, high), jnp.where(core == 0, high, mixed)


def exchange(values, axis, second, flip):
    axes = tuple(name for name in AXES if name in ("core", axis))
    number = (lambda core, at: 2 * at + core) if axis == "x" else (lambda core, at: RING * core + at)
    pairs = []
    for core in range(2):
        for at in range(RING):
            other = at ^ 1 if core ^ flip == second else RING - 1 - at
            pairs.append((number(core, at), number(core, other)))
    return lax.ppermute(values, axes, pairs)


def add(*terms):
    return functools.reduce(jnp.add, [t.astype(jnp.float32) for t in terms])


def sum_flow(keep, send, axes, flip):
    first, last = axes
    come = [exchange(send, first, 0, flip[0])]
    for axis, second in ((first, 1), (last, 0), (last, 1)):
        terms = [keep] + come
        terms = [t[(0,) * (t.ndim - come[-1].ndim)][1] for t in terms]
        come.append(exchange(add(*terms).astype(keep.dtype), axis, second, flip[axis == last]))
    return add(*[t[(0,) * (t.ndim - 3)] for t in [keep] + come])


def product_kernel(flow, count, based, gates, steps, where, *refs):
    slabs, refs = refs[:count], refs[count:]
    base, outs, left = refs[:based], refs[based + gates : -1], refs[-1]
    last = flow is not None

    def block(n):
        return jnp.concatenate([slab[n] for slab in slabs], axis=0)

    def run(flow, _):
        begin, pairs = flow * steps[0], steps[flow]
        rows, parity = steps[2 + 2 * flow], steps[3 + 2 * flow]

        def turn(n, _):
            turned = block(n).T
            for g in range(BLK // PART):
                left[n, g ^ rows] = turned[g * PART : (g + 1) * PART]
            return 0

        def some(m, _):
            for n in range(UNROLL):
                u = jnp.minimum(UNROLL * m + n, pairs - 1)
                for k in range(2):
                    code = where[2 * (begin + u) + (k ^ parity)]
                    lhs = left[code & 255].reshape(BLK, -1)
                    full = jnp.dot(lhs, block((code >> 8) & 255), preferred_element_type=jnp.float32)
                    if based:
                        full += base[0][begin + u, k]
                    if last:
                        full = full.reshape(2, 2, 2, PART, BLK).astype(jnp.bfloat16)
                        outs[0][:, :, k, u] = full[0]
                        outs[1][:, :, k, u] = full[1]
                    else:
                        outs[0][begin + u, k] = full
            return 0

        @pl.when(pairs > 0)
        def _():
            low = (where[2 * begin] >> 16) & 255
            high = where[2 * (begin + pairs) - 1] >> 24
            lax.fori_loop(low, high + 1, turn, 0)
            lax.fori_loop(0, (pairs + UNROLL - 1) // UNROLL, some, 0)

        return 0

    if last:
        run(flow, 0)
    else:
        lax.fori_loop(0, 2, run, 0)


def products(flow, steps, where, slabs, room, base=None, gate=()):
    blocks, rows, _ = slabs[0].shape
    pairs = room // 2
    whole = jax.ShapeDtypeStruct((pairs, 2, BLK, BLK), jnp.float32)
    part = pairs if flow is None else pairs - late_share(pairs) if flow else late_share(pairs)
    half = jax.ShapeDtypeStruct((2, 2, 2, part, PART, BLK), jnp.bfloat16)
    extra = [] if base is None else [base]
    depth = len(slabs) * rows
    need = 2 * 2 * blocks * depth * BLK + 2 * pairs * BLK * BLK * (6 if extra else 2 if flow is not None else 4) + 4 * 2**20
    return pl.pallas_call(
        functools.partial(product_kernel, flow, len(slabs), len(extra), len(gate)),
        out_shape=whole if flow is None else (half, half),
        in_specs=[SMEM] * 2 + [VMEM] * (len(slabs) + len(extra)) + [ANY] * len(gate),
        out_specs=VMEM if flow is None else (VMEM, VMEM),
        scratch_shapes=[pltpu.VMEM((blocks, BLK // PART, PART, depth), jnp.bfloat16)],
        compiler_params=pltpu.CompilerParams(vmem_limit_bytes=need),
        cost_estimate=pl.CostEstimate(flops=10**4, bytes_accessed=10**4, transcendentals=0),
        name="products",
    )(steps, where, *slabs, *extra, *gate)


def energy_kernel(steps, what, partners, pair_count, eps_occ, *refs):
    sums, eps_rows, (eps_lanes, out, acc, lines) = refs[:2], refs[2:4], refs[4:]
    acc[...] = jnp.zeros_like(acc)
    for flow in range(2):

        def step(m, _, flow=flow):
            for n in range(UNROLL):
                u = jnp.minimum(UNROLL * m + n, steps[flow] - 1)
                code = what[2 * (flow * steps[0] + u) + steps[3 + 2 * flow]]
                pair = jnp.where(UNROLL * m + n < steps[flow], code & 511, NONE)
                real = jnp.minimum(pair, NONE - 1)
                i, j = real // NOCC, real % NOCC
                value = sums[flow][u]
                bottom = eps_rows[flow][(code >> 9) & 31] + eps_lanes[pl.ds(code >> 14, 1), :] - eps_occ[i] - eps_occ[j]
                term = value * value / bottom
                acc[pair] += term[: PART // 2] + term[PART // 2 :]
            return 0

        lax.fori_loop(0, (steps[flow] + UNROLL - 1) // UNROLL, step, 0)

    def line(i, _):
        lanes = []
        for p in range(NPAIR):
            j = partners[p, i]
            pair = jnp.where(p < pair_count[i], jnp.minimum(i, j) * NOCC + jnp.maximum(i, j), NONE + 1)
            lanes.append(jnp.sum(acc[pair], axis=0, keepdims=True))
        lines[i] = jnp.concatenate(lanes, axis=0)
        return 0

    lax.fori_loop(0, NOCC, line, 0)
    table = -jnp.sum(lines[...], axis=2)
    table = jnp.concatenate([table, jnp.zeros((NOCC, BLK - NPAIR), jnp.float32)], axis=1)
    for n in range(out.shape[0]):
        out[n] = table


def energies(steps, what, partners, pair_count, eps_occ, sums, eps_rows, eps_lanes):
    return pl.pallas_call(
        energy_kernel,
        out_shape=jax.ShapeDtypeStruct((COPIES, NOCC, BLK), jnp.float32),
        in_specs=[SMEM] * 5 + [VMEM] * 5,
        out_specs=VMEM,
        scratch_shapes=[
            pltpu.VMEM((NONE + 8, PART // 2, BLK), jnp.float32),
            pltpu.VMEM((NOCC, NPAIR, BLK), jnp.float32),
        ],
        compiler_params=pltpu.CompilerParams(vmem_limit_bytes=8 * sums[0].size + 6 * 2**20),
        name="energies",
    )(steps, what, partners, pair_count, eps_occ, *sums, *eps_rows, eps_lanes)


def body(b_factors, eps_occ, eps_virt, dom_blocks, dom_count, partners, pair_count):
    blocks, partners = dom_blocks.T, partners.T
    rank = lax.axis_index(SHARE).astype(jnp.int32).reshape(1)
    info, first, mask = make_sizes(dom_count, partners, pair_count)

    (first_x, second_x), (first_y, second_y) = place("x", FLIPS[0][0]), place("y", FLIPS[0][1])
    (later_y, last_y), (later_x, last_x) = place("y", FLIPS[1][0]), place("x", FLIPS[1][1])
    rows = (4 * first_x + 2 * second_x + first_y, 4 * later_y + 2 * last_y + later_x)
    mine = jnp.stack([rows[0], second_y, rows[1], last_x]).astype(jnp.int32)
    eps_lanes = eps_virt.reshape(-1, BLK)

    def branch(sizes):
        blocks_room, tiles_room = sizes
        split = tiles_room < 256

        def beside(twin):
            info_then, _ = lax.optimization_barrier((info, twin))
            plan = make_plan(info_then, first, mask, dom_count, blocks, rank, mine)
            eps_rows = [lax.dynamic_slice_in_dim(eps_lanes, r * PART, PART, axis=1) for r in rows]
            return plan, [jnp.broadcast_to(e[:, :, None], e.shape + (BLK,)) for e in eps_rows]

        def early(pieces, extra, gate):
            (steps, where, _), _ = extra
            return products(None, steps, where, pieces, tiles_room, gate=[gate]) if split else None

        own = select(dom_count, blocks, b_factors, blocks_room)
        pieces, late, ((steps, where, what), eps_rows), done = gather(own, beside, early)
        late = late if split else pieces + late
        sums = []
        for flow, axes in enumerate((("x", "y"), ("y", "x"))):
            keep, send = products(flow, steps, where, late, tiles_room, base=done)
            sums.append(sum_flow(keep, send, axes, FLIPS[flow]))
        return energies(steps, what, partners, pair_count, eps_occ, sums, eps_rows, eps_lanes)

    table = lax.switch(info[0], [functools.partial(branch, sizes) for sizes in SIZES])
    came = lax.all_to_all(table.reshape(COPIES * NOCC, BLK), AXES, split_axis=0, concat_axis=0, tiled=True)
    return jnp.sum(came, axis=0, keepdims=True)[:, :NPAIR]


def solution(mesh):
    fine = Mesh(mesh.devices.reshape(4, 2, 4, 4), AXES)
    return jax.shard_map(
        body,
        mesh=fine,
        in_specs=(P(None, AXES, None), P(), P(), P(), P(), P(), P()),
        out_specs=P(("y", "z"), None),
        check_vma=False,
    )
```

```python
import functools

import jax
import jax.numpy as jnp
from jax import lax
from jax.experimental import pallas as pl
from jax.experimental.pallas import tpu as pltpu
from jax.sharding import Mesh
from jax.sharding import PartitionSpec as P

BLK = 128
MAXDOM = 6
NPAIR = 8
NOCC = 16
AXES = ("x", "core", "y", "z")
SHARE = ("core", "z")
NSHARE = 8
RING = 4
FLIPS = ((0, 0), (1, 0))
COPIES = 8
NSUM = 16
PART = 2 * BLK // NSUM
SIZES = ((58, 90), (65, 122), (73, 172), (96, 576))
MAXTILE = SIZES[-1][1]
UNROLL = 4
NONE = NOCC * NOCC

SMEM = pl.BlockSpec(memory_space=pltpu.SMEM)
VMEM = pl.BlockSpec(memory_space=pltpu.VMEM)
ANY = pl.BlockSpec(memory_space=pl.ANY)


def sizes_kernel(count, partners, pair_count, info, first, mask):
    live_blocks = jnp.int32(0)
    for i in range(NOCC):
        first[i] = live_blocks
        mask[i] = 0
        live_blocks = live_blocks + count[i]

    for i in range(NOCC):
        for p in range(NPAIR):

            @pl.when(p < pair_count[i])
            def _(i=i, p=p):
                j = partners[p, i]
                low, high = jnp.minimum(i, j), jnp.maximum(i, j)
                mask[low] = mask[low] | (jnp.int32(1) << high)

    tiles = jnp.int32(0)
    for i in range(NOCC):
        row = mask[i]
        width = jnp.int32(0)
        for j in range(i, NOCC):
            width = width + ((row >> j) & 1) * count[j]
        tiles = tiles + width * count[i]
    quota = 2 * ((tiles + 2 * NSHARE - 1) // (2 * NSHARE))
    branch = jnp.int32(len(SIZES) - 1)
    for n in reversed(range(len(SIZES) - 1)):
        fits = (live_blocks <= SIZES[n][0]) & (quota <= SIZES[n][1])
        branch = jnp.where(fits, n, branch)
    info[0] = branch
    info[1] = quota
    info[2] = tiles


def make_sizes(count, partners, pair_count):
    return pl.pallas_call(
        sizes_kernel,
        out_shape=(
            jax.ShapeDtypeStruct((4,), jnp.int32),
            jax.ShapeDtypeStruct((NOCC,), jnp.int32),
            jax.ShapeDtypeStruct((NOCC,), jnp.int32),
        ),
        in_specs=[SMEM] * 3,
        out_specs=(SMEM, SMEM, SMEM),
        name="sizes",
    )(count, partners, pair_count)


def late_share(pairs):
    return pairs // 2


def plan_kernel(info, first, mask, count, blocks, rank, mine, steps, where, what):
    low_tile = rank[0] * info[1]
    high_tile = jnp.minimum(low_tile + info[1], info[2])

    def left(i, start):
        def right(j, start):
            width = count[j]
            size = jnp.where(((mask[i] >> j) & 1) == 1, count[i] * width, 0)

            @pl.when((start < high_tile) & (start + size > low_tile))
            def _():
                span = (first[i] << 16) | ((first[i] + count[i] - 1) << 24)

                def row(s, begin):
                    lo = jnp.maximum(low_tile - begin, 0)
                    hi = jnp.minimum(high_tile - begin, width)

                    def tile(t, _):
                        n = begin + t - low_tile
                        where[n] = (first[i] + s) | ((first[j] + t) << 8) | span
                        what[n] = (i * NOCC + j) | (blocks[s, i] << 9) | (blocks[t, j] << 14)
                        return 0

                    lax.fori_loop(lo, hi, tile, 0)
                    return begin + width

                lax.fori_loop(0, count[i], row, start)

            return start + size

        return lax.fori_loop(i, NOCC, right, start)

    lax.fori_loop(0, NOCC, left, jnp.int32(0))
    tiles = jnp.maximum(high_tile - low_tile, 0)

    pairs = (tiles + 1) // 2

    @pl.when(tiles % 2 == 1)
    def _():
        where[tiles] = where[tiles - 1]
        what[tiles] = NONE

    steps[0] = late_share(pairs)
    steps[1] = pairs - late_share(pairs)
    for n in range(4):
        steps[2 + n] = mine[n]


def make_plan(info, first, mask, count, blocks, rank, mine):
    return pl.pallas_call(
        plan_kernel,
        out_shape=(
            jax.ShapeDtypeStruct((6,), jnp.int32),
            jax.ShapeDtypeStruct((MAXTILE,), jnp.int32),
            jax.ShapeDtypeStruct((MAXTILE,), jnp.int32),
        ),
        in_specs=[SMEM] * 7,
        out_specs=(SMEM, SMEM, SMEM),
        cost_estimate=pl.CostEstimate(flops=10**7, bytes_accessed=10**7, transcendentals=0),
        name="plan",
    )(info, first, mask, count, blocks, rank, mine)


def select_kernel(count, blocks, factors, picked, sem):
    def left(i, live):
        for s in range(MAXDOM):

            @pl.when(s < count[i])
            def _(s=s):
                column = pl.multiple_of(blocks[s, i] * BLK, BLK)
                pltpu.make_async_copy(factors.at[i, :, pl.ds(column, BLK)], picked.at[live + s], sem).start()

        return live + count[i]

    live = lax.fori_loop(0, NOCC, left, jnp.int32(0))
    room = picked.shape[0]
    for bit in range(room.bit_length()):

        @pl.when((live >> bit) & 1 == 1)
        def _(bit=bit):
            some = picked.at[pl.ds(0, 1 << bit)]
            pltpu.make_async_copy(some, some, sem).wait()


def select(count, blocks, factors, room):
    rows = factors.shape[1]
    return pl.pallas_call(
        select_kernel,
        out_shape=jax.ShapeDtypeStruct((room, rows, BLK), factors.dtype),
        in_specs=[SMEM, SMEM, ANY],
        out_specs=VMEM,
        scratch_shapes=[pltpu.SemaphoreType.DMA],
        compiler_params=pltpu.CompilerParams(vmem_limit_bytes=8 * 2**20),
        name="select",
    )(count, blocks, factors)


def gather(own, beside, early):
    swap = [(0, 1), (1, 0)]
    around = [(RING * c + z, RING * c + (z + 1 - 2 * c) % RING) for c in range(2) for z in range(RING)]
    twin = lax.ppermute(own, "core", swap)
    near = lax.ppermute(own, SHARE, around)
    near_twin = lax.ppermute(twin, SHARE, around)
    near, extra = lax.optimization_barrier((near, beside(twin)))
    far = lax.ppermute(near, SHARE, around)
    pieces = [own, twin, near, lax.ppermute(near, "core", swap), near_twin]
    gate = lax.ppermute(near_twin[:1], "core", swap)
    done = early(pieces, extra, gate)
    far, done = lax.optimization_barrier((far, done))
    return pieces, [lax.ppermute(near_twin, "core", swap), far, lax.ppermute(far, "core", swap)], extra, done


def place(axis, flip):
    core, at = lax.axis_index("core") ^ flip, lax.axis_index(axis)
    high, mixed = at >> 1, (at >> 1) ^ (at & 1)
    return jnp.where(core == 0, mixed, high), jnp.where(core == 0, high, mixed)


def exchange(values, axis, second, flip):
    axes = tuple(name for name in AXES if name in ("core", axis))
    number = (lambda core, at: 2 * at + core) if axis == "x" else (lambda core, at: RING * core + at)
    pairs = []
    for core in range(2):
        for at in range(RING):
            other = at ^ 1 if core ^ flip == second else RING - 1 - at
            pairs.append((number(core, at), number(core, other)))
    return lax.ppermute(values, axes, pairs)


def add(*terms):
    return functools.reduce(jnp.add, [t.astype(jnp.float32) for t in terms])


def sum_flow(keep, send, axes, flip):
    first, last = axes
    come = [exchange(send, first, 0, flip[0])]
    for axis, second in ((first, 1), (last, 0), (last, 1)):
        terms = [keep] + come
        terms = [t[(0,) * (t.ndim - come[-1].ndim)][1] for t in terms]
        come.append(exchange(add(*terms).astype(keep.dtype), axis, second, flip[axis == last]))
    return add(*[t[(0,) * (t.ndim - 3)] for t in [keep] + come])


def product_kernel(flow, count, based, gates, steps, where, *refs):
    slabs, refs = refs[:count], refs[count:]
    base, outs, left = refs[:based], refs[based + gates : -1], refs[-1]
    last = flow is not None

    def block(n):
        return jnp.concatenate([slab[n] for slab in slabs], axis=0)

    def run(flow, _):
        begin, pairs = flow * steps[0], steps[flow]
        rows, parity = steps[2 + 2 * flow], steps[3 + 2 * flow]

        def turn(n, _):
            turned = block(n).T
            for g in range(BLK // PART):
                left[n, g ^ rows] = turned[g * PART : (g + 1) * PART]
            return 0

        wide = 8 if last else UNROLL

        def some(m, _):
            for n in range(wide):
                u = jnp.minimum(wide * m + n, pairs - 1)
                for k in range(2):
                    code = where[2 * (begin + u) + (k ^ parity)]
                    lhs = left[code & 255].reshape(BLK, -1)
                    full = jnp.dot(lhs, block((code >> 8) & 255), preferred_element_type=jnp.float32)
                    if based:
                        full += base[0][begin + u, k]
                    if last:
                        full = full.reshape(2, 2, 2, PART, BLK).astype(jnp.bfloat16)
                        outs[0][:, :, k, u] = full[0]
                        outs[1][:, :, k, u] = full[1]
                    else:
                        outs[0][begin + u, k] = full
            return 0

        @pl.when(pairs > 0)
        def _():
            low = (where[2 * begin] >> 16) & 255
            high = where[2 * (begin + pairs) - 1] >> 24
            lax.fori_loop(low, high + 1, turn, 0)
            lax.fori_loop(0, (pairs + wide - 1) // wide, some, 0)

        return 0

    if last:
        run(flow, 0)
    else:
        lax.fori_loop(0, 2, run, 0)


def products(flow, steps, where, slabs, room, base=None, gate=()):
    blocks, rows, _ = slabs[0].shape
    pairs = room // 2
    whole = jax.ShapeDtypeStruct((pairs, 2, BLK, BLK), jnp.float32)
    part = pairs if flow is None else pairs - late_share(pairs) if flow else late_share(pairs)
    half = jax.ShapeDtypeStruct((2, 2, 2, part, PART, BLK), jnp.bfloat16)
    extra = [] if base is None else [base]
    depth = len(slabs) * rows
    need = 2 * 2 * blocks * depth * BLK + 2 * pairs * BLK * BLK * (6 if extra else 2 if flow is not None else 4) + 4 * 2**20
    return pl.pallas_call(
        functools.partial(product_kernel, flow, len(slabs), len(extra), len(gate)),
        out_shape=whole if flow is None else (half, half),
        in_specs=[SMEM] * 2 + [VMEM] * (len(slabs) + len(extra)) + [ANY] * len(gate),
        out_specs=VMEM if flow is None else (VMEM, VMEM),
        scratch_shapes=[pltpu.VMEM((blocks, BLK // PART, PART, depth), jnp.bfloat16)],
        compiler_params=pltpu.CompilerParams(vmem_limit_bytes=need),
        cost_estimate=pl.CostEstimate(flops=10**4, bytes_accessed=10**4, transcendentals=0),
        name="products",
    )(steps, where, *slabs, *extra, *gate)


def energy_kernel(steps, what, partners, pair_count, eps_occ, *refs):
    sums, eps_rows, (eps_lanes, out, acc, lines) = refs[:2], refs[2:4], refs[4:]
    acc[...] = jnp.zeros_like(acc)
    for flow in range(2):

        def step(m, _, flow=flow):
            for n in range(UNROLL):
                u = jnp.minimum(UNROLL * m + n, steps[flow] - 1)
                code = what[2 * (flow * steps[0] + u) + steps[3 + 2 * flow]]
                pair = jnp.where(UNROLL * m + n < steps[flow], code & 511, NONE)
                real = jnp.minimum(pair, NONE - 1)
                i, j = real // NOCC, real % NOCC
                value = sums[flow][u]
                bottom = eps_rows[flow][(code >> 9) & 31] + eps_lanes[pl.ds(code >> 14, 1), :] - eps_occ[i] - eps_occ[j]
                term = value * value / bottom
                acc[pair] += term[: PART // 2] + term[PART // 2 :]
            return 0

        lax.fori_loop(0, (steps[flow] + UNROLL - 1) // UNROLL, step, 0)

    def line(i, _):
        lanes = []
        for p in range(NPAIR):
            j = partners[p, i]
            pair = jnp.where(p < pair_count[i], jnp.minimum(i, j) * NOCC + jnp.maximum(i, j), NONE + 1)
            lanes.append(jnp.sum(acc[pair], axis=0, keepdims=True))
        lines[i] = jnp.concatenate(lanes, axis=0)
        return 0

    lax.fori_loop(0, NOCC, line, 0)
    table = -jnp.sum(lines[...], axis=2)
    table = jnp.concatenate([table, jnp.zeros((NOCC, BLK - NPAIR), jnp.float32)], axis=1)
    for n in range(out.shape[0]):
        out[n] = table


def energies(steps, what, partners, pair_count, eps_occ, sums, eps_rows, eps_lanes):
    return pl.pallas_call(
        energy_kernel,
        out_shape=jax.ShapeDtypeStruct((COPIES, NOCC, BLK), jnp.float32),
        in_specs=[SMEM] * 5 + [VMEM] * 5,
        out_specs=VMEM,
        scratch_shapes=[
            pltpu.VMEM((NONE + 8, PART // 2, BLK), jnp.float32),
            pltpu.VMEM((NOCC, NPAIR, BLK), jnp.float32),
        ],
        compiler_params=pltpu.CompilerParams(vmem_limit_bytes=8 * sums[0].size + 6 * 2**20),
        name="energies",
    )(steps, what, partners, pair_count, eps_occ, *sums, *eps_rows, eps_lanes)


def body(b_factors, eps_occ, eps_virt, dom_blocks, dom_count, partners, pair_count):
    blocks, partners = dom_blocks.T, partners.T
    rank = lax.axis_index(SHARE).astype(jnp.int32).reshape(1)
    info, first, mask = make_sizes(dom_count, partners, pair_count)

    (first_x, second_x), (first_y, second_y) = place("x", FLIPS[0][0]), place("y", FLIPS[0][1])
    (later_y, last_y), (later_x, last_x) = place("y", FLIPS[1][0]), place("x", FLIPS[1][1])
    rows = (4 * first_x + 2 * second_x + first_y, 4 * later_y + 2 * last_y + later_x)
    mine = jnp.stack([rows[0], second_y, rows[1], last_x]).astype(jnp.int32)
    eps_lanes = eps_virt.reshape(-1, BLK)

    def branch(sizes):
        blocks_room, tiles_room = sizes
        split = tiles_room < 256

        def beside(twin):
            info_then, _ = lax.optimization_barrier((info, twin))
            plan = make_plan(info_then, first, mask, dom_count, blocks, rank, mine)
            eps_rows = [lax.dynamic_slice_in_dim(eps_lanes, r * PART, PART, axis=1) for r in rows]
            return plan, [jnp.broadcast_to(e[:, :, None], e.shape + (BLK,)) for e in eps_rows]

        def early(pieces, extra, gate):
            (steps, where, _), _ = extra
            return products(None, steps, where, pieces, tiles_room, gate=[gate]) if split else None

        own = select(dom_count, blocks, b_factors, blocks_room)
        pieces, late, ((steps, where, what), eps_rows), done = gather(own, beside, early)
        late = late if split else pieces + late
        sums = []
        for flow, axes in enumerate((("x", "y"), ("y", "x"))):
            keep, send = products(flow, steps, where, late, tiles_room, base=done)
            sums.append(sum_flow(keep, send, axes, FLIPS[flow]))
        return energies(steps, what, partners, pair_count, eps_occ, sums, eps_rows, eps_lanes)

    table = lax.switch(info[0], [functools.partial(branch, sizes) for sizes in SIZES])
    came = lax.all_to_all(table.reshape(COPIES * NOCC, BLK), AXES, split_axis=0, concat_axis=0, tiled=True)
    return jnp.sum(came, axis=0, keepdims=True)[:, :NPAIR]


def solution(mesh):
    fine = Mesh(mesh.devices.reshape(4, 2, 4, 4), AXES)
    return jax.shard_map(
        body,
        mesh=fine,
        in_specs=(P(None, AXES, None), P(), P(), P(), P(), P(), P()),
        out_specs=P(("y", "z"), None),
        check_vma=False,
    )
```

```python
import functools

import jax
import jax.numpy as jnp
from jax import lax
from jax.experimental import pallas as pl
from jax.experimental.pallas import tpu as pltpu
from jax.sharding import Mesh
from jax.sharding import PartitionSpec as P

BLK = 128
MAXDOM = 6
NPAIR = 8
NOCC = 16
AXES = ("x", "core", "y", "z")
SHARE = ("core", "z")
NSHARE = 8
RING = 4
FLIPS = ((0, 0), (1, 0))
COPIES = 8
NSUM = 16
PART = 2 * BLK // NSUM
SIZES = ((58, 90), (65, 122), (73, 172), (96, 576))
MAXTILE = SIZES[-1][1]
UNROLL = 4
NONE = NOCC * NOCC

SMEM = pl.BlockSpec(memory_space=pltpu.SMEM)
VMEM = pl.BlockSpec(memory_space=pltpu.VMEM)
ANY = pl.BlockSpec(memory_space=pl.ANY)


def sizes_kernel(count, partners, pair_count, info, first, mask):
    live_blocks = jnp.int32(0)
    for i in range(NOCC):
        first[i] = live_blocks
        mask[i] = 0
        live_blocks = live_blocks + count[i]

    for i in range(NOCC):
        for p in range(NPAIR):

            @pl.when(p < pair_count[i])
            def _(i=i, p=p):
                j = partners[p, i]
                low, high = jnp.minimum(i, j), jnp.maximum(i, j)
                mask[low] = mask[low] | (jnp.int32(1) << high)

    tiles = jnp.int32(0)
    for i in range(NOCC):
        row = mask[i]
        width = jnp.int32(0)
        for j in range(i + 1, NOCC):
            width = width + ((row >> j) & 1) * count[j]
        tiles = tiles + width * count[i] + ((row >> i) & 1) * (count[i] * (count[i] + 1) // 2)
    quota = 2 * ((tiles + 2 * NSHARE - 1) // (2 * NSHARE))
    branch = jnp.int32(len(SIZES) - 1)
    for n in reversed(range(len(SIZES) - 1)):
        fits = (live_blocks <= SIZES[n][0]) & (quota <= SIZES[n][1])
        branch = jnp.where(fits, n, branch)
    info[0] = branch
    info[1] = quota
    info[2] = tiles


def make_sizes(count, partners, pair_count):
    return pl.pallas_call(
        sizes_kernel,
        out_shape=(
            jax.ShapeDtypeStruct((4,), jnp.int32),
            jax.ShapeDtypeStruct((NOCC,), jnp.int32),
            jax.ShapeDtypeStruct((NOCC,), jnp.int32),
        ),
        in_specs=[SMEM] * 3,
        out_specs=(SMEM, SMEM, SMEM),
        name="sizes",
    )(count, partners, pair_count)


def late_share(pairs):
    return pairs // 2


def plan_kernel(info, first, mask, count, blocks, rank, mine, steps, where, what):
    low_tile = rank[0] * info[1]
    high_tile = jnp.minimum(low_tile + info[1], info[2])

    def left(i, start):
        def right(j, start):
            width = count[j]
            own = jnp.where(i == j, 1, 0)
            size = jnp.where(i == j, width * (width + 1) // 2, count[i] * width)
            size = jnp.where(((mask[i] >> j) & 1) == 1, size, 0)

            @pl.when((start < high_tile) & (start + size > low_tile))
            def _():
                span = (first[i] << 16) | ((first[i] + count[i] - 1) << 24)

                def row(s, begin):
                    lo = jnp.maximum(low_tile - begin, 0)
                    skip = own * s
                    hi = jnp.minimum(high_tile - begin, width - skip)

                    def tile(m, _):
                        n, t = begin + m - low_tile, m + skip
                        twice = jnp.where((own == 1) & (s < t), 1 << 19, 0)
                        where[n] = (first[i] + s) | ((first[j] + t) << 8) | span
                        what[n] = (i * NOCC + j) | (blocks[s, i] << 9) | (blocks[t, j] << 14) | twice
                        return 0

                    lax.fori_loop(lo, hi, tile, 0)
                    return begin + width - skip

                lax.fori_loop(0, count[i], row, start)

            return start + size

        return lax.fori_loop(i, NOCC, right, start)

    lax.fori_loop(0, NOCC, left, jnp.int32(0))
    tiles = jnp.maximum(high_tile - low_tile, 0)

    pairs = (tiles + 1) // 2

    @pl.when(tiles % 2 == 1)
    def _():
        where[tiles] = where[tiles - 1]
        what[tiles] = NONE

    steps[0] = late_share(pairs)
    steps[1] = pairs - late_share(pairs)
    for n in range(4):
        steps[2 + n] = mine[n]


def make_plan(info, first, mask, count, blocks, rank, mine):
    return pl.pallas_call(
        plan_kernel,
        out_shape=(
            jax.ShapeDtypeStruct((6,), jnp.int32),
            jax.ShapeDtypeStruct((MAXTILE,), jnp.int32),
            jax.ShapeDtypeStruct((MAXTILE,), jnp.int32),
        ),
        in_specs=[SMEM] * 7,
        out_specs=(SMEM, SMEM, SMEM),
        cost_estimate=pl.CostEstimate(flops=10**7, bytes_accessed=10**7, transcendentals=0),
        name="plan",
    )(info, first, mask, count, blocks, rank, mine)


def select_kernel(count, blocks, factors, picked, sem):
    def left(i, live):
        for s in range(MAXDOM):

            @pl.when(s < count[i])
            def _(s=s):
                column = pl.multiple_of(blocks[s, i] * BLK, BLK)
                pltpu.make_async_copy(factors.at[i, :, pl.ds(column, BLK)], picked.at[live + s], sem).start()

        return live + count[i]

    live = lax.fori_loop(0, NOCC, left, jnp.int32(0))
    room = picked.shape[0]
    for bit in range(room.bit_length()):

        @pl.when((live >> bit) & 1 == 1)
        def _(bit=bit):
            some = picked.at[pl.ds(0, 1 << bit)]
            pltpu.make_async_copy(some, some, sem).wait()


def select(count, blocks, factors, room):
    rows = factors.shape[1]
    return pl.pallas_call(
        select_kernel,
        out_shape=jax.ShapeDtypeStruct((room, rows, BLK), factors.dtype),
        in_specs=[SMEM, SMEM, ANY],
        out_specs=VMEM,
        scratch_shapes=[pltpu.SemaphoreType.DMA],
        compiler_params=pltpu.CompilerParams(vmem_limit_bytes=8 * 2**20),
        name="select",
    )(count, blocks, factors)


def gather(own, beside, early):
    swap = [(0, 1), (1, 0)]
    around = [(RING * c + z, RING * c + (z + 1 - 2 * c) % RING) for c in range(2) for z in range(RING)]
    twin = lax.ppermute(own, "core", swap)
    near = lax.ppermute(own, SHARE, around)
    near_twin = lax.ppermute(twin, SHARE, around)
    near, extra = lax.optimization_barrier((near, beside(twin)))
    far = lax.ppermute(near, SHARE, around)
    pieces = [own, twin, near, lax.ppermute(near, "core", swap), near_twin]
    gate = lax.ppermute(near_twin[:1], "core", swap)
    done = early(pieces, extra, gate)
    far, done = lax.optimization_barrier((far, done))
    return pieces, [lax.ppermute(near_twin, "core", swap), far, lax.ppermute(far, "core", swap)], extra, done


def place(axis, flip):
    core, at = lax.axis_index("core") ^ flip, lax.axis_index(axis)
    high, mixed = at >> 1, (at >> 1) ^ (at & 1)
    return jnp.where(core == 0, mixed, high), jnp.where(core == 0, high, mixed)


def exchange(values, axis, second, flip):
    axes = tuple(name for name in AXES if name in ("core", axis))
    number = (lambda core, at: 2 * at + core) if axis == "x" else (lambda core, at: RING * core + at)
    pairs = []
    for core in range(2):
        for at in range(RING):
            other = at ^ 1 if core ^ flip == second else RING - 1 - at
            pairs.append((number(core, at), number(core, other)))
    return lax.ppermute(values, axes, pairs)


def add(*terms):
    return functools.reduce(jnp.add, [t.astype(jnp.float32) for t in terms])


def sum_flow(keep, send, axes, flip):
    first, last = axes
    come = [exchange(send, first, 0, flip[0])]
    for axis, second in ((first, 1), (last, 0), (last, 1)):
        terms = [keep] + come
        terms = [t[(0,) * (t.ndim - come[-1].ndim)][1] for t in terms]
        come.append(exchange(add(*terms).astype(keep.dtype), axis, second, flip[axis == last]))
    return add(*[t[(0,) * (t.ndim - 3)] for t in [keep] + come])


def product_kernel(flow, count, based, gates, steps, where, *refs):
    slabs, refs = refs[:count], refs[count:]
    base, outs, left = refs[:based], refs[based + gates : -1], refs[-1]
    last = flow is not None

    def block(n):
        return jnp.concatenate([slab[n] for slab in slabs], axis=0)

    def run(flow, _):
        begin, pairs = flow * steps[0], steps[flow]
        rows, parity = steps[2 + 2 * flow], steps[3 + 2 * flow]

        def turn(n, _):
            turned = block(n).T
            for g in range(BLK // PART):
                left[n, g ^ rows] = turned[g * PART : (g + 1) * PART]
            return 0

        wide = 8 if last else UNROLL

        def some(m, _):
            for n in range(wide):
                u = jnp.minimum(wide * m + n, pairs - 1)
                for k in range(2):
                    code = where[2 * (begin + u) + (k ^ parity)]
                    lhs = left[code & 255].reshape(BLK, -1)
                    full = jnp.dot(lhs, block((code >> 8) & 255), preferred_element_type=jnp.float32)
                    if based:
                        full += base[0][begin + u, k]
                    if last:
                        full = full.reshape(2, 2, 2, PART, BLK).astype(jnp.bfloat16)
                        outs[0][:, :, k, u] = full[0]
                        outs[1][:, :, k, u] = full[1]
                    else:
                        outs[0][begin + u, k] = full
            return 0

        @pl.when(pairs > 0)
        def _():
            low = (where[2 * begin] >> 16) & 255
            high = where[2 * (begin + pairs) - 1] >> 24
            lax.fori_loop(low, high + 1, turn, 0)
            lax.fori_loop(0, (pairs + wide - 1) // wide, some, 0)

        return 0

    if last:
        run(flow, 0)
    else:
        lax.fori_loop(0, 2, run, 0)


def products(flow, steps, where, slabs, room, base=None, gate=()):
    blocks, rows, _ = slabs[0].shape
    pairs = room // 2
    whole = jax.ShapeDtypeStruct((pairs, 2, BLK, BLK), jnp.float32)
    part = pairs if flow is None else pairs - late_share(pairs) if flow else late_share(pairs)
    half = jax.ShapeDtypeStruct((2, 2, 2, part, PART, BLK), jnp.bfloat16)
    extra = [] if base is None else [base]
    depth = len(slabs) * rows
    need = 2 * 2 * blocks * depth * BLK + 2 * pairs * BLK * BLK * (6 if extra else 2 if flow is not None else 4) + 4 * 2**20
    return pl.pallas_call(
        functools.partial(product_kernel, flow, len(slabs), len(extra), len(gate)),
        out_shape=whole if flow is None else (half, half),
        in_specs=[SMEM] * 2 + [VMEM] * (len(slabs) + len(extra)) + [ANY] * len(gate),
        out_specs=VMEM if flow is None else (VMEM, VMEM),
        scratch_shapes=[pltpu.VMEM((blocks, BLK // PART, PART, depth), jnp.bfloat16)],
        compiler_params=pltpu.CompilerParams(vmem_limit_bytes=need),
        cost_estimate=pl.CostEstimate(flops=10**4, bytes_accessed=10**4, transcendentals=0),
        name="products",
    )(steps, where, *slabs, *extra, *gate)


def energy_kernel(steps, what, partners, pair_count, eps_occ, *refs):
    sums, eps_rows, (eps_lanes, out, acc, lines) = refs[:2], refs[2:4], refs[4:]
    acc[...] = jnp.zeros_like(acc)
    for flow in range(2):

        def step(m, _, flow=flow):
            for n in range(UNROLL):
                u = jnp.minimum(UNROLL * m + n, steps[flow] - 1)
                code = what[2 * (flow * steps[0] + u) + steps[3 + 2 * flow]]
                pair = jnp.where(UNROLL * m + n < steps[flow], code & 511, NONE)
                real = jnp.minimum(pair, NONE - 1)
                i, j = real // NOCC, real % NOCC
                value = sums[flow][u]
                bottom = eps_rows[flow][(code >> 9) & 31] + eps_lanes[pl.ds((code >> 14) & 31, 1), :] - eps_occ[i] - eps_occ[j]
                term = value * value / bottom * jnp.where(code >> 19 == 1, 2.0, 1.0)
                acc[pair] += term[: PART // 2] + term[PART // 2 :]
            return 0

        lax.fori_loop(0, (steps[flow] + UNROLL - 1) // UNROLL, step, 0)

    def line(i, _):
        lanes = []
        for p in range(NPAIR):
            j = partners[p, i]
            pair = jnp.where(p < pair_count[i], jnp.minimum(i, j) * NOCC + jnp.maximum(i, j), NONE + 1)
            lanes.append(jnp.sum(acc[pair], axis=0, keepdims=True))
        lines[i] = jnp.concatenate(lanes, axis=0)
        return 0

    lax.fori_loop(0, NOCC, line, 0)
    table = -jnp.sum(lines[...], axis=2)
    table = jnp.concatenate([table, jnp.zeros((NOCC, BLK - NPAIR), jnp.float32)], axis=1)
    for n in range(out.shape[0]):
        out[n] = table


def energies(steps, what, partners, pair_count, eps_occ, sums, eps_rows, eps_lanes):
    return pl.pallas_call(
        energy_kernel,
        out_shape=jax.ShapeDtypeStruct((COPIES, NOCC, BLK), jnp.float32),
        in_specs=[SMEM] * 5 + [VMEM] * 5,
        out_specs=VMEM,
        scratch_shapes=[
            pltpu.VMEM((NONE + 8, PART // 2, BLK), jnp.float32),
            pltpu.VMEM((NOCC, NPAIR, BLK), jnp.float32),
        ],
        compiler_params=pltpu.CompilerParams(vmem_limit_bytes=8 * sums[0].size + 6 * 2**20),
        name="energies",
    )(steps, what, partners, pair_count, eps_occ, *sums, *eps_rows, eps_lanes)


def body(b_factors, eps_occ, eps_virt, dom_blocks, dom_count, partners, pair_count):
    blocks, partners = dom_blocks.T, partners.T
    rank = lax.axis_index(SHARE).astype(jnp.int32).reshape(1)
    info, first, mask = make_sizes(dom_count, partners, pair_count)

    (first_x, second_x), (first_y, second_y) = place("x", FLIPS[0][0]), place("y", FLIPS[0][1])
    (later_y, last_y), (later_x, last_x) = place("y", FLIPS[1][0]), place("x", FLIPS[1][1])
    rows = (4 * first_x + 2 * second_x + first_y, 4 * later_y + 2 * last_y + later_x)
    mine = jnp.stack([rows[0], second_y, rows[1], last_x]).astype(jnp.int32)
    eps_lanes = eps_virt.reshape(-1, BLK)

    def branch(sizes):
        blocks_room, tiles_room = sizes
        split = tiles_room < 256

        def beside(twin):
            info_then, _ = lax.optimization_barrier((info, twin))
            plan = make_plan(info_then, first, mask, dom_count, blocks, rank, mine)
            eps_rows = [lax.dynamic_slice_in_dim(eps_lanes, r * PART, PART, axis=1) for r in rows]
            return plan, [jnp.broadcast_to(e[:, :, None], e.shape + (BLK,)) for e in eps_rows]

        def early(pieces, extra, gate):
            (steps, where, _), _ = extra
            return products(None, steps, where, pieces, tiles_room, gate=[gate]) if split else None

        own = select(dom_count, blocks, b_factors, blocks_room)
        pieces, late, ((steps, where, what), eps_rows), done = gather(own, beside, early)
        late = late if split else pieces + late
        sums = []
        for flow, axes in enumerate((("x", "y"), ("y", "x"))):
            keep, send = products(flow, steps, where, late, tiles_room, base=done)
            sums.append(sum_flow(keep, send, axes, FLIPS[flow]))
        return energies(steps, what, partners, pair_count, eps_occ, sums, eps_rows, eps_lanes)

    table = lax.switch(info[0], [functools.partial(branch, sizes) for sizes in SIZES])
    came = lax.all_to_all(table.reshape(COPIES * NOCC, BLK), AXES, split_axis=0, concat_axis=0, tiled=True)
    return jnp.sum(came, axis=0, keepdims=True)[:, :NPAIR]


def solution(mesh):
    fine = Mesh(mesh.devices.reshape(4, 2, 4, 4), AXES)
    return jax.shard_map(
        body,
        mesh=fine,
        in_specs=(P(None, AXES, None), P(), P(), P(), P(), P(), P()),
        out_specs=P(("y", "z"), None),
        check_vma=False,
    )
```
